512 devices in a mesh: gz: 64 (over x, y, core), gy: 8 (over z).
Axes of the slice: x: 4, y: 8, z: 8, core: 2. Of those that a mesh axis runs over, the one named last changes fastest.
Arguments:
- velocity_u: float32 [2, 1536, 8192], P(None, 'gy', 'gz'), may hold values from -6 to 6
- velocity_v: float32 [2, 1536, 8192], P(None, 'gy', 'gz'), may hold values from -6 to 6
- velocity_w: float32 [2, 1536, 8192], P(None, 'gy', 'gz'), may hold values from -6 to 6
- stiffness: float32 [2, 1536, 8192], P(None, 'gy', 'gz'), may hold values from 10 to 1000
- w_in: float32 [3, 128], replicated, may hold values from -3.5 to 3.5
- b_in: float32 [128], replicated, may hold values from -3 to 3
- w_mid: float32 [128, 128], replicated, may hold values from -0.5 to 0.5
- b_mid: float32 [128], replicated, may hold values from -3 to 3
- w_out: float32 [128], replicated, may hold values from -0.5 to 0.5
- cell_list: int32 [2, 262144], P(None, 'gz'), may hold values from 0 to 255
- height_list: int32 [2, 262144], P(None, 'gz'), may hold values from 1 to 8
- face_list: int32 [2, 262144], P(None, 'gz'), may hold values from 0 to 255
- owner_list: int32 [2, 262144, 1], P(None, 'gz'), may hold values from 0 to 63; in each aligned block of 4096 rows (0 to 4095, 4096 to 8191, ..., all dimensions but the last counted through in order) at most 128 rows name the same one
Outputs:
- new_u: float32 [2, 1536, 8192], P(None, 'gy', 'gz')
The draws below stay inside these ranges and needn't reach their ends.
Inputs may be any that keep to these rules, and one draw needn't show every extreme that they name: `owner_list`: in each aligned block of 4096 rows of one wall (the rows of one device) no owner is named by more than 128 rows, a bound that some block reaches.
All inputs are finite; a program needn't handle non-finite values.
Results may differ from the reference program's by a relative error of at most 0.000067.
Values sent between devices are 32-bit elements; how exact they have to be, the bound alone decides.
A program may use at most 64 MiB of HBM per device.

```python
import math
import jax
import jax.numpy as jnp
import numpy as np
from jax import lax

X = 2
CZ = 128
ROWS = 4096
HMAX = 8
HID = 128
NY = 1536
NZ = 8192
CAP = 128
FACES = 256
N_GZ = 64


def place_ends(drawn, key, least, high):
    longest = drawn.shape.index(max(drawn.shape))
    spots = []
    for shift in (0, 1):
        where = [jax.random.randint(jax.random.fold_in(key, axis), (), 0, length) for axis, length in enumerate(drawn.shape)]
        where[longest] = (where[longest] + shift) % drawn.shape[longest]
        spots.append(tuple(where))
    return drawn.at[spots[0]].set(least).at[spots[1]].set(high)


def level_of(rng, dims, shards, least, high):
    def one(dim, blocks):
        steps = jax.random.uniform(jax.random.fold_in(jax.random.fold_in(rng, 6), dim), (blocks,), jnp.float32, least / len(shards), high / len(shards))
        return jnp.repeat(jnp.exp(steps), dims[dim] // blocks).reshape((-1,) + (1,) * (len(dims) - dim - 1))

    factor_of = one(*shards[0])
    for cut in shards[1:]:
        factor_of = factor_of * one(*cut)
    return factor_of


def deal_out(key, own, number, rows, amount, top, bound, slope):
    order = jax.random.permutation(key, amount)
    heavy_load, ordinary = load_shares(amount, rows * top, bound, slope, True), load_shares(amount, rows * top, bound, slope, False)
    places = jnp.arange(amount)

    def named(sizes, offset_by):
        used = int((sizes > 0).sum())
        fixed = max(1, used // 4)
        shifted = fixed + (places - fixed + offset_by * (used - fixed)) % max(1, amount - fixed)
        return jnp.zeros((amount,), jnp.int32).at[order[jnp.where(places < fixed, places, shifted)]].set(jnp.asarray(sizes, jnp.int32))

    sizes = jnp.where(number % 4 == 0, named(heavy_load, number // 4), named(ordinary, number - number // 4 - 1))
    mixed = jax.random.permutation(jax.random.fold_in(own, 3), amount)
    giver, receiver = mixed[0:amount // 2 * 2:2], mixed[1:amount // 2 * 2:2]
    slack = jnp.minimum(sizes[giver] - 1, bound - sizes[receiver]) // 2
    slack = jnp.where((giver == order[0]) | (receiver == order[0]) | (sizes[receiver] == 0), 0, jnp.maximum(slack, 0))
    shifted = jax.random.randint(jax.random.fold_in(own, 4), (amount // 2,), 0, 1 << 20) % (slack + 1)
    sizes = sizes.at[giver].add(-shifted).at[receiver].add(shifted)
    members = jnp.searchsorted(jnp.cumsum(sizes), jnp.arange(rows * top), side="right").astype(jnp.int32)
    table = members.reshape(top, rows).T
    table = table[jax.random.permutation(jax.random.fold_in(own, 1), rows)]
    offset_by = jax.random.randint(jax.random.fold_in(own, 2), (rows, 1), 0, top)
    return jnp.take_along_axis(table, (jnp.arange(top)[None, :] + offset_by) % top, axis=1)


def load_shares(number_of, total, bound, lean, full):
    weights = [(1 << 20) // math.isqrt(standing ** lean) + 1 for standing in range(1, number_of + 1)]
    largest = bound if full else min(bound, max(-(-total // number_of), total * weights[0] // sum(weights)))
    least = 1 if total - largest >= number_of - 1 else 0
    counts, spare = [largest] + [least] * (number_of - 1), total - largest - least * (number_of - 1)
    while spare > 0:
        free = [i for i in range(1, number_of) if counts[i] < largest] or [i for i in range(1, number_of) if counts[i] < bound]
        whole, left = sum([weights[i] for i in free]), spare
        for i in free:
            extra = min(bound - counts[i], max(1, left * weights[i] // whole), spare)
            counts[i] = counts[i] + extra
            spare = spare - extra
    return np.array(counts)


def bell_draw(stream_key, shape, spread, most, pieces=(), kind=jnp.bfloat16):
    values = spread * jax.random.normal(stream_key, shape, jnp.float32)
    if pieces:
        values = values * level_of(stream_key, shape, pieces, -0.22, 0.18)
    return jnp.clip(values, -most, most).astype(kind)


def setup_inputs(seed: int = 0) -> dict:
    arg_keys = jax.random.split(jax.random.key(seed), 14)
    velocity_u = bell_draw(arg_keys[0], (X, NY, NZ), 1.0, 6.0, ((1, 8), (2, 64)), jnp.float32)
    velocity_v = bell_draw(arg_keys[1], (X, NY, NZ), 1.0, 6.0, ((1, 8), (2, 64)), jnp.float32)
    velocity_w = bell_draw(arg_keys[2], (X, NY, NZ), 1.0, 6.0, ((1, 8), (2, 64)), jnp.float32)
    stiffness = jnp.clip(jnp.exp(math.log(1000.0) - 4.6051702 * jax.random.uniform(arg_keys[3], (X, NY, NZ), jnp.float32) ** level_of(arg_keys[3], (X, NY, NZ), ((1, 8), (2, 64)), -0.2, 0.2)), 10.0, 1000.0)
    w_in = bell_draw(arg_keys[4], (3, HID), 3 ** -0.5, 3.5, (), jnp.float32)
    b_in = bell_draw(arg_keys[5], (HID,), 0.5, 3.0, (), jnp.float32)
    w_mid = bell_draw(arg_keys[6], (HID, HID), HID ** -0.5, 0.5, (), jnp.float32)
    b_mid = bell_draw(arg_keys[7], (HID,), 0.5, 3.0, (), jnp.float32)
    w_out = bell_draw(arg_keys[8], (HID,), HID ** -0.5, 0.5, (), jnp.float32)
    cell_list = place_ends(jax.random.randint(arg_keys[9], (2, ROWS * N_GZ), 0, X * CZ), jax.random.fold_in(arg_keys[9], 1), 0, (X * CZ) - 1).astype(jnp.int32)
    height_list = place_ends(jax.random.randint(arg_keys[10], (2, ROWS * N_GZ), 1, HMAX + 1), jax.random.fold_in(arg_keys[10], 1), 1, HMAX).astype(jnp.int32)
    face_list = place_ends(jax.random.randint(arg_keys[11], (2, ROWS * N_GZ), 0, X * CZ), jax.random.fold_in(arg_keys[11], 1), 0, (X * CZ) - 1).astype(jnp.int32)
    owner_list_keys = jax.random.split(jax.random.fold_in(arg_keys[12], 1), 2 * (ROWS * N_GZ) // ROWS)
    owner_list_turns = jax.random.permutation(jax.random.fold_in(arg_keys[12], 3), 2 * (ROWS * N_GZ) // ROWS)
    owner_list = jax.vmap(lambda own, number: deal_out(jax.random.fold_in(arg_keys[12], 2), own, number, ROWS, N_GZ, 1, CAP, 2))(owner_list_keys, owner_list_turns).reshape((2, ROWS * N_GZ, 1))
    return {"velocity_u": velocity_u, "velocity_v": velocity_v, "velocity_w": velocity_w, "stiffness": stiffness, "w_in": w_in, "b_in": b_in, "w_mid": w_mid, "b_mid": b_mid, "w_out": w_out, "cell_list": cell_list, "height_list": height_list, "face_list": face_list, "owner_list": owner_list}


def stress_net(inputs, w_in, b_in, w_mid, b_mid, w_out):
    highest = lax.Precision.HIGHEST
    hidden = jnp.tanh(jnp.dot(w_in.T, inputs, precision=highest) + b_in[:, None])
    hidden = jnp.tanh(jnp.dot(w_mid.T, hidden, precision=highest) + b_mid[:, None])
    return jnp.dot(w_out, hidden, precision=highest)


def reference(velocity_u, velocity_v, velocity_w, stiffness, w_in, b_in, w_mid, b_mid, w_out, cell_list, height_list, face_list, owner_list):
    total_rows = ROWS * N_GZ
    source_dev = jnp.arange(total_rows, dtype=jnp.int32) // ROWS
    plane_idx = cell_list // CZ
    span_idx = source_dev[None, :] * CZ + cell_list % CZ
    level_idx = jnp.stack([height_list[0], NY - 1 - height_list[1]])
    sample = jnp.stack([velocity_u[plane_idx, level_idx, span_idx], velocity_v[plane_idx, level_idx, span_idx], velocity_w[plane_idx, level_idx, span_idx]])
    blocks = jnp.transpose(sample.reshape(3, 2 * N_GZ, ROWS), (1, 0, 2))
    row_stress = lax.map(lambda block: stress_net(block, w_in, b_in, w_mid, b_mid, w_out), blocks).reshape(-1)
    wall_base = (jnp.arange(2, dtype=jnp.int32) * (N_GZ * FACES))[:, None]
    face_key = (owner_list[:, :, 0] * FACES + face_list + wall_base).reshape(-1)
    total = jax.ops.segment_sum(row_stress, face_key, 2 * N_GZ * FACES)
    count = jax.ops.segment_sum(jnp.ones_like(row_stress), face_key, 2 * N_GZ * FACES)
    wall_stress = total / jnp.maximum(count, 1.0)
    wall_stress = jnp.transpose(wall_stress.reshape(2, N_GZ, X, CZ), (0, 2, 1, 3)).reshape(2, X, NZ)
    lateral = jnp.roll(velocity_u, 1, 2) + jnp.roll(velocity_u, -1, 2) - 2.0 * velocity_u
    source = velocity_u + 0.2 * lateral
    source = source.at[:, 0, :].add(wall_stress[0] * (1.0 + stiffness[:, 0, :]))
    source = source.at[:, NY - 1, :].add(wall_stress[1] * (1.0 + stiffness[:, NY - 1, :]))
    gain = 1.0 / (1.0 + stiffness)
    keep = stiffness * gain
    keep_rows = jnp.moveaxis(keep, 1, 0)
    gain_rows = jnp.moveaxis(gain, 1, 0)
    source_rows = jnp.moveaxis(source, 1, 0)

    def forward_step(carry, items):
        value = items[0] * carry + items[1] * items[2]
        return value, value

    start = jnp.zeros((X, NZ), velocity_u.dtype)
    _, forward_val = lax.scan(forward_step, start, (keep_rows, gain_rows, source_rows))
    _, result_rows = lax.scan(forward_step, start, (keep_rows, gain_rows, forward_val), reverse=True)
    return jnp.moveaxis(result_rows, 0, 1)
```

```python
import functools

import jax
import jax.numpy as jnp
from jax import lax
from jax.experimental import pallas as pl
from jax.experimental.pallas import tpu as pltpu
from jax.sharding import PartitionSpec as P

MESH = pl.DeviceIdType.MESH
LANES = 128
SUB = 8
WIN = 16
HMAX = 8
KB = 512
F32 = jnp.float32
BF16 = jnp.bfloat16


def load_rows(ref, p, b, steps):
    return ref[p, pl.ds(b, SUB, stride=steps), :]


def step_loop(count, unroll, body, init):
    def outer(i, carry):
        for j in range(unroll):
            carry = body(i * unroll + j, carry)
        return carry

    return lax.fori_loop(0, count // unroll, outer, init)


def kernel(
    gz,
    gy,
    nx,
    u_hbm,
    v_hbm,
    w_hbm,
    s_hbm,
    w_in_hbm,
    b_in_hbm,
    w_mid_hbm,
    b_mid_hbm,
    w_out_hbm,
    cell_hbm,
    height_hbm,
    face_hbm,
    owner_hbm,
    bl_out,
    q_out,
    fb_out,
    f_out,
    b_out,
    u_ref,
    s_ref,
    win_ref,
    w_in_ref,
    vec_ref,
    w_mid_ref,
    cell_ref,
    height_ref,
    face_ref,
    owner_ref,
    cols_ref,
    wl_ref,
    samp_ref,
    table_ref,
    acc_ref,
    keep_ref,
    gain_ref,
    gsrc_ref,
    lf_ref,
    ff_ref,
    bl_ref,
    q_ref,
    fb_ref,
    edge_ref,
    pack_ref,
    halo_ref,
    send_a,
    recv_a,
    send_b,
    recv_b,
    send_s,
    recv_s,
    load_sem,
    out_sem,
    halo_send,
    halo_recv,
    a_send,
    a_recv,
    b_send,
    b_recv,
    s_send,
    s_recv,
):
    planes, levels, _ = u_ref.shape
    steps = levels // SUB
    total_steps = planes * steps
    nyc = gz // nx
    roles = (0, 1, gy - 2, gy - 1)
    me = lax.axis_index("gz")
    level = lax.axis_index("gy")
    xx = me // nyc
    yc = me % nyc
    is_top = level >= gy // 2
    is_tot = (level == 0) | (level == gy - 1)
    is_role = is_tot | (level == 1) | (level == gy - 2)
    role = jnp.where(is_top, level - (gy - 4), level)

    start = pl.multiple_of(jnp.where(is_top, levels - WIN, 0), 8)
    load_u = pltpu.make_async_copy(u_hbm, u_ref, load_sem.at[0])
    load_s = pltpu.make_async_copy(s_hbm, s_ref, load_sem.at[1])
    lists = [
        pltpu.make_async_copy(src, dst, load_sem.at[2 + i])
        for i, (src, dst) in enumerate(
            [(cell_hbm, cell_ref), (height_hbm, height_ref), (face_hbm, face_ref), (owner_hbm, owner_ref)]
        )
    ]
    weights = [
        pltpu.make_async_copy(src, dst, load_sem.at[6 + i])
        for i, (src, dst) in enumerate(
            [
                (w_in_hbm, w_in_ref),
                (b_in_hbm, vec_ref.at[0]),
                (b_mid_hbm, vec_ref.at[1]),
                (w_out_hbm, vec_ref.at[2]),
                (w_mid_hbm, w_mid_ref),
                (v_hbm.at[:, pl.ds(start, WIN), :], win_ref.at[0]),
                (w_hbm.at[:, pl.ds(start, WIN), :], win_ref.at[1]),
            ]
        )
    ]
    load_u.start()

    @pl.when(is_tot)
    def _():
        for copy in weights:
            copy.start()

    @pl.when(is_role)
    def _():
        for copy in lists:
            copy.start()

    load_s.start()

    barrier = pltpu.get_barrier_semaphore()

    def greet(z, y):
        pl.semaphore_signal(barrier, inc=1, device_id=(z, y), device_id_type=MESH)

    left, right = lax.rem(me + gz - 1, gz), lax.rem(me + 1, gz)
    greet(left, level)
    greet(right, level)

    @pl.loop(1, gy)
    def _(d):
        greet(me, lax.rem(level + d, gy))

    @pl.loop(1, nx)
    def _(d):
        for r in roles:
            greet(lax.rem(xx + d, nx) * nyc + yc, r)

    @pl.when(is_role)
    def _():
        @pl.loop(1, nyc)
        def _(d):
            greet(xx * nyc + lax.rem(yc + d, nyc), level)

    lane = lax.broadcasted_iota(jnp.int32, (SUB, LANES), 1)
    row = lax.broadcasted_iota(jnp.int32, (SUB, LANES), 0)
    load_u.wait()
    packed = jnp.zeros((SUB, LANES), F32)
    for p in range(planes):

        def pack(b, acc, p=p):
            i = p * steps + b
            return jnp.where(lane // 2 == i, pltpu.roll(load_rows(u_ref, p, b, steps), 2 * i + 1, 1), acc)

        packed = step_loop(steps, 8, pack, packed)
    pack_ref[...] = packed

    base = gy - 1 + 2

    @pl.when(is_role)
    def _():
        pl.semaphore_wait(barrier, base + nyc - 1 + (nx - 1) * gy)

    @pl.when(jnp.logical_not(is_role))
    def _():
        pl.semaphore_wait(barrier, base)

    halo_copies = [
        pltpu.make_async_remote_copy(
            src_ref=pack_ref,
            dst_ref=halo_ref.at[slot],
            send_sem=halo_send.at[slot],
            recv_sem=halo_recv.at[slot],
            device_id=(z, level),
            device_id_type=MESH,
        )
        for slot, z in ((0, right), (1, left))
    ]
    for copy in halo_copies:
        copy.start()

    def copy_a(z, slot):
        return pltpu.make_async_remote_copy(
            src_ref=send_a.at[z],
            dst_ref=recv_a.at[slot],
            send_sem=a_send,
            recv_sem=a_recv,
            device_id=(xx * nyc + z, level),
            device_id_type=MESH,
        )

    def copy_b(x, y):
        return pltpu.make_async_remote_copy(
            src_ref=send_b.at[x],
            dst_ref=recv_b.at[role * nx + xx],
            send_sem=b_send,
            recv_sem=b_recv,
            device_id=(x * nyc + yc, y),
            device_id_type=MESH,
        )

    def copy_s(y):
        return pltpu.make_async_remote_copy(
            src_ref=send_s,
            dst_ref=recv_s.at[level],
            send_sem=s_send,
            recv_sem=s_recv,
            device_id=(me, y),
            device_id_type=MESH,
        )

    @pl.when(is_tot)
    def _():
        for copy in weights:
            copy.wait()
        vectors = jnp.concatenate(
            [w_in_ref[...], vec_ref[0], vec_ref[1], vec_ref[2], jnp.zeros((2, LANES), F32)], axis=0
        )
        columns = vectors.T
        for c in range(6):
            cols_ref[c] = jnp.broadcast_to(columns[:, c : c + 1], (LANES, LANES))
        mid = w_mid_ref[...].T
        mid_hi = mid.astype(BF16)
        mid_lo = (mid - mid_hi.astype(F32)).astype(BF16)
        wl_ref[...] = jnp.concatenate(
            [jnp.concatenate([mid_hi, mid_hi], axis=1), jnp.concatenate([mid_lo, mid_lo], axis=1)], axis=0
        )
        for p in range(planes):
            samp_ref[0, p * HMAX : (p + 1) * HMAX, :] = jnp.where(
                is_top, u_ref[p, levels - 1 - HMAX : levels - 1, :], u_ref[p, 1 : 1 + HMAX, :]
            )
            for c in range(2):
                samp_ref[1 + c, p * HMAX : (p + 1) * HMAX, :] = jnp.where(
                    is_top, win_ref[c, p, WIN - 1 - HMAX : WIN - 1, :], win_ref[c, p, 1 : 1 + HMAX, :]
                )

        @pl.loop(0, planes * HMAX // 2)
        def _(i):
            halves = []
            for h in range(2):
                k = i * 2 + h
                pre = cols_ref[3]
                for c in range(3):
                    pre = pre + cols_ref[c] * samp_ref[c, pl.ds(k, 1), :]
                hidden = jnp.tanh(pre)
                upper = hidden.astype(BF16)
                lower = (hidden - upper.astype(F32)).astype(BF16)
                halves.append(jnp.concatenate([upper, lower], axis=0))
            mixed = jnp.dot(wl_ref[...], jnp.concatenate(halves, axis=1), preferred_element_type=F32)
            for h in range(2):
                part = mixed[:, h * LANES : (h + 1) * LANES]
                second = jnp.tanh(part[:LANES] + part[LANES:] + cols_ref[4])
                table_ref[pl.ds(i * 2 + h, 1), :] = jnp.sum(second * cols_ref[5], axis=0, keepdims=True)

    @pl.when(is_role & jnp.logical_not(is_tot))
    def _():
        table_ref[...] = jnp.ones_like(table_ref)

    @pl.when(is_role)
    def _():
        for copy in lists:
            copy.wait()
        rows = cell_ref.shape[1]
        acc_ref[...] = jnp.zeros_like(acc_ref)
        bins = acc_ref.shape[0]
        rows_iota = lax.broadcasted_iota(jnp.int32, (LANES, KB), 0)
        bins_iota = lax.broadcasted_iota(jnp.int32, (bins, KB), 0)

        @pl.loop(0, rows // KB)
        def _(i):
            at = pl.ds(pl.multiple_of(i * KB, KB), KB)

            def wall(ref):
                return jnp.where(is_top, ref[1:2, at], ref[0:1, at])

            cell, height, face = wall(cell_ref), wall(height_ref), wall(face_ref)
            owner = owner_ref[:, pl.ds(pl.multiple_of(jnp.where(is_top, rows, 0) + i * KB, KB), KB)]
            span = cell % LANES
            key = (cell // LANES) * HMAX + jnp.where(is_top, HMAX - height, height - 1)
            picks = []
            for j in range(KB // LANES):
                cut = slice(j * LANES, (j + 1) * LANES)
                index = jnp.broadcast_to(span[:, cut], (SUB, LANES))
                keyed = jnp.broadcast_to(key[:, cut], (SUB, LANES))
                value = jnp.zeros((SUB, LANES), F32)
                for t in range(planes):
                    got = jnp.take_along_axis(table_ref[t * HMAX : (t + 1) * HMAX, :], index, axis=1)
                    value = value + jnp.where(keyed == row + t * HMAX, got, 0.0)
                picks.append(jnp.sum(value, axis=0, keepdims=True))
            value = jnp.concatenate(picks, axis=1)
            first = value.astype(BF16).astype(F32)
            rest = value - first
            low = face % LANES
            high = (owner % nyc) * (2 * nx) + (owner // nyc) * 2 + face // LANES
            onto = jnp.where(bins_iota == high, 1.0, 0.0).astype(BF16)
            named = rows_iota == low
            carried = jnp.concatenate(
                [jnp.where(named, first, 0.0).astype(BF16), jnp.where(named, rest, 0.0).astype(BF16)], axis=0
            )
            acc_ref[...] += lax.dot_general(
                onto, carried, (((1,), (1,)), ((), ())), preferred_element_type=F32
            )

        binned = acc_ref[:, :LANES] + acc_ref[:, LANES:]
        send_a[...] = binned.reshape(send_a.shape)
        recv_a[yc] = send_a[yc]

        @pl.loop(1, nyc)
        def _(d):
            copy_a(lax.rem(yc + d, nyc), yc).start()

    load_s.wait()
    for copy in halo_copies:
        copy.wait_recv()
    merged = jnp.where(lane % 2 == 1, pltpu.roll(halo_ref[0], 1, 1), pltpu.roll(halo_ref[1], LANES - 1, 1))
    zero, one = jnp.zeros((SUB, LANES), F32), jnp.ones((SUB, LANES), F32)
    summaries = []
    for p in range(planes):

        def prepare(b, _, p=p):
            i = p * steps + b
            stiff = load_rows(s_ref, p, b, steps)
            here = load_rows(u_ref, p, b, steps)
            halo = pltpu.roll(merged, LANES - 1 - 2 * i, 1)
            before = jnp.where(lane == 0, halo, pltpu.roll(here, 1, 1))
            after = jnp.where(lane == LANES - 1, halo, pltpu.roll(here, LANES - 1, 1))
            source = here + 0.2 * (after + before - 2.0 * here)
            gain = 1.0 / (1.0 + stiff)
            keep_ref[p, b] = stiff * gain
            gain_ref[p, b] = gain
            gsrc_ref[p, b] = gain * source
            return _

        step_loop(steps, 4, prepare, 0)

    def forward(b, carry):
        out = []
        for p in range(planes):
            value, factor = carry[2 * p : 2 * p + 2]
            keep = keep_ref[p, b]
            value = keep * value + gsrc_ref[p, b]
            factor = keep * factor
            lf_ref[p, b] = value
            ff_ref[p, b] = factor
            out += [value, factor]
        return tuple(out)

    forwards = step_loop(steps, 4, forward, (zero, one) * planes)

    def backward(t, carry):
        out = []
        b = steps - 1 - t
        for p in range(planes):
            value, response, factor = carry[3 * p : 3 * p + 3]
            keep, gain = keep_ref[p, b], gain_ref[p, b]
            value = keep * value + gain * lf_ref[p, b]
            response = keep * response + gain * ff_ref[p, b]
            factor = keep * factor
            at = pl.ds(b, SUB, stride=steps)
            bl_ref[p, at, :] = value
            q_ref[p, at, :] = response
            fb_ref[p, at, :] = factor
            out += [value, response, factor]
        return tuple(out)

    backwards = step_loop(steps, 4, backward, (zero, zero, one) * planes)
    outs = [
        pltpu.make_async_copy(src, dst, out_sem.at[i])
        for i, (src, dst) in enumerate([(bl_ref, bl_out), (q_ref, q_out), (fb_ref, fb_out)])
    ]
    for copy in outs:
        copy.start()

    inner = []
    for p in range(planes):
        local_f = forwards[2 * p]
        local_b, response, product = backwards[3 * p : 3 * p + 3]
        pi, li = product, local_f
        for d in (1, 2, 4):
            ok = row >= d
            lp = jnp.where(ok, pltpu.roll(li, d, 0), 0.0)
            pp = jnp.where(ok, pltpu.roll(pi, d, 0), 1.0)
            li, pi = pi * lp + li, pi * pp
        pf = jnp.where(row >= 1, pltpu.roll(pi, 1, 0), 1.0)
        lf = jnp.where(row >= 1, pltpu.roll(li, 1, 0), 0.0)
        pb, cb, qb = product, local_b + response * lf, response * pf
        for d in (1, 2, 4):
            ok = row < SUB - d
            cp = jnp.where(ok, pltpu.roll(cb, SUB - d, 0), 0.0)
            qp = jnp.where(ok, pltpu.roll(qb, SUB - d, 0), 0.0)
            pp = jnp.where(ok, pltpu.roll(pb, SUB - d, 0), 1.0)
            cb, qb, pb = pb * cp + cb, pb * qp + qb, pb * pp
        ok = row < SUB - 1
        summaries.append((pb[0:1], li[SUB - 1 : SUB], cb[0:1], qb[0:1]))
        inner.append(
            (
                pf,
                lf,
                jnp.where(ok, pltpu.roll(pb, SUB - 1, 0), 1.0),
                jnp.where(ok, pltpu.roll(cb, SUB - 1, 0), 0.0),
                jnp.where(ok, pltpu.roll(qb, SUB - 1, 0), 0.0),
            )
        )
    own_alpha = jnp.concatenate([1.0 / keep_ref[p, 0, 0:1] for p in range(planes)], axis=0)
    own_eps = jnp.concatenate([1.0 / s_ref[p, levels - 1 : levels, :] for p in range(planes)], axis=0)
    at_bottom, at_top = level == 0, level == gy - 1
    blocks = [jnp.concatenate([summaries[p][c] for p in range(planes)], axis=0) for c in range(4)]
    blocks[0] = blocks[0] * jnp.where(at_bottom, own_alpha, jnp.where(at_top, own_eps, 1.0))
    summary = jnp.concatenate(blocks, axis=0)
    send_s[...] = summary
    recv_s[level] = summary

    @pl.loop(1, gy)
    def _(d):
        copy_s(lax.rem(level + d, gy)).start()

    @pl.when(is_role)
    def _():
        pltpu.make_async_copy(recv_a.at[pl.ds(0, nyc - 1)], recv_a.at[pl.ds(0, nyc - 1)], a_recv).wait()
        part = recv_a[0]
        for i in range(1, nyc):
            part = part + recv_a[i]
        for x in range(nx):
            send_b[x] = part[2 * x : 2 * x + 2, :]
        recv_b[role * nx + xx] = send_b[xx]

        @pl.loop(1, nx * gy)
        def _(d):
            flat = lax.rem(xx * gy + level + d, nx * gy)
            copy_b(flat // gy, flat % gy).start()

    pltpu.make_async_copy(recv_s.at[pl.ds(0, gy - 1)], recv_s.at[pl.ds(0, gy - 1)], s_recv).wait()

    def block(g, c):
        return recv_s[g, 2 * c : 2 * c + 2, :]

    alphas, betas = [None, block(0, 0)], [None, block(0, 1)]
    for g in range(1, gy - 1):
        alphas.append(block(g, 0) * alphas[g])
        betas.append(block(g, 0) * betas[g] + block(g, 1))
    alpha, beta = jnp.where(at_bottom, own_alpha, 0.0), jnp.zeros_like(own_alpha)
    for g in range(1, gy):
        alpha = jnp.where(level == g, alphas[g], alpha)
        beta = jnp.where(level == g, betas[g], beta)
    top = gy - 1
    gam, dlt, eps = block(top, 3) * alphas[top], block(top, 2) + block(top, 3) * betas[top], block(top, 0)
    gamma, delta = jnp.zeros_like(own_alpha), jnp.zeros_like(own_alpha)
    epsilon = jnp.where(at_top, own_eps, 0.0)
    for g in range(gy - 2, -1, -1):
        gamma = jnp.where(level == g, gam, gamma)
        delta = jnp.where(level == g, dlt, delta)
        epsilon = jnp.where(level == g, eps, epsilon)
        if g:
            gam = block(g, 0) * gam + block(g, 3) * alphas[g]
            dlt = block(g, 0) * dlt + block(g, 2) + block(g, 3) * betas[g]
            eps = block(g, 0) * eps

    count = 4 * nx

    @pl.when(is_role)
    def _():
        pltpu.make_async_copy(recv_b.at[pl.ds(0, count - 1)], recv_b.at[pl.ds(0, count - 1)], b_recv).wait()

    @pl.when(jnp.logical_not(is_role))
    def _():
        pltpu.make_async_copy(recv_b, recv_b, b_recv).wait()

    sums = []
    for r in range(4):
        total = recv_b[r * nx]
        for x in range(1, nx):
            total = total + recv_b[r * nx + x]
        sums.append(total)
    stress_low = sums[0] / jnp.maximum(sums[1], 1.0)
    stress_top = sums[3] / jnp.maximum(sums[2], 1.0)
    f_in = alpha * stress_low + beta
    b_in = gamma * stress_low + delta + epsilon * stress_top
    for p in range(planes):
        pf, lf, pb, cb, qb = inner[p]
        edge_ref[0, p] = pf * f_in[p : p + 1] + lf
        edge_ref[1, p] = pb * b_in[p : p + 1] + cb + qb * f_in[p : p + 1]
    edges = [
        pltpu.make_async_copy(edge_ref.at[i], dst, out_sem.at[3 + i]) for i, dst in enumerate([f_out, b_out])
    ]
    for copy in edges:
        copy.start()

    for copy in halo_copies:
        copy.wait_send()
    pltpu.make_async_copy(recv_s.at[pl.ds(0, gy - 1)], recv_s.at[pl.ds(0, gy - 1)], s_send).wait()

    @pl.when(is_role)
    def _():
        pltpu.make_async_copy(send_a.at[pl.ds(0, nyc - 1)], send_a.at[pl.ds(0, nyc - 1)], a_send).wait()
        for _ in range(gy - 1):
            pltpu.make_async_copy(send_b, send_b, b_send).wait()
        pltpu.make_async_copy(send_b.at[pl.ds(0, nx - 1)], send_b.at[pl.ds(0, nx - 1)], b_send).wait()

    for copy in outs + edges:
        copy.wait()


def local(gz, gy, nx, *args):
    u, v, w, s, w_in, b_in, w_mid, b_mid, w_out, cell, height, face, owner = args
    planes, levels, span = u.shape
    steps = levels // SUB
    nyc = gz // nx
    rows = cell.shape[1]
    field = jax.ShapeDtypeStruct(u.shape, F32)
    vmem = pltpu.VMEM
    scratch = [
        vmem(u.shape, F32),
        vmem(u.shape, F32),
        vmem((2, planes, WIN, span), F32),
        vmem((3, span), F32),
        vmem((3, 1, span), F32),
        vmem((span, span), F32),
        vmem((2, rows), jnp.int32),
        vmem((2, rows), jnp.int32),
        vmem((2, rows), jnp.int32),
        vmem((1, 2 * rows), jnp.int32),
        vmem((6, span, span), F32),
        vmem((2 * span, 2 * span), BF16),
        vmem((3, planes * HMAX, span), F32),
        vmem((planes * HMAX, span), F32),
        vmem((2 * gz, 2 * span), F32),
        vmem((planes, steps, SUB, span), F32),
        vmem((planes, steps, SUB, span), F32),
        vmem((planes, steps, SUB, span), F32),
        vmem((planes, steps, SUB, span), F32),
        vmem((planes, steps, SUB, span), F32),
        vmem(u.shape, F32),
        vmem(u.shape, F32),
        vmem(u.shape, F32),
        vmem((2, planes, SUB, span), F32),
        vmem((SUB, span), F32),
        vmem((2, SUB, span), F32),
        vmem((nyc, 2 * nx, span), F32),
        vmem((nyc, 2 * nx, span), F32),
        vmem((nx, 2, span), F32),
        vmem((4 * nx, 2, span), F32),
        vmem((8, span), F32),
        vmem((gy, 8, span), F32),
        pltpu.SemaphoreType.DMA((13,)),
        pltpu.SemaphoreType.DMA((5,)),
        pltpu.SemaphoreType.DMA((2,)),
        pltpu.SemaphoreType.DMA((2,)),
    ] + [pltpu.SemaphoreType.DMA] * 6
    bl, q, fb, below, above = pl.pallas_call(
        functools.partial(kernel, gz, gy, nx),
        out_shape=[field] * 3 + [jax.ShapeDtypeStruct((planes, SUB, span), F32)] * 2,
        in_specs=[pl.BlockSpec(memory_space=pl.ANY)] * 13,
        out_specs=[pl.BlockSpec(memory_space=pl.ANY)] * 5,
        scratch_shapes=scratch,
        compiler_params=pltpu.CompilerParams(
            collective_id=0, has_side_effects=True, vmem_limit_bytes=63 * 2**20
        ),
    )(
        u,
        v,
        w,
        s,
        w_in,
        b_in[None, :],
        w_mid,
        b_mid[None, :],
        w_out[None, :],
        cell,
        height,
        face,
        owner.reshape(1, 2 * rows),
    )
    shape = (planes, SUB, steps, span)
    out = bl.reshape(shape) + q.reshape(shape) * below[:, :, None, :] + fb.reshape(shape) * above[:, :, None, :]
    return out.reshape(u.shape)


def solution(mesh):
    field = P(None, "gy", "gz")
    gz, gy = mesh.shape["gz"], mesh.shape["gy"]
    return jax.shard_map(
        functools.partial(local, gz, gy, 4),
        mesh=mesh,
        in_specs=(field,) * 4 + (P(),) * 5 + (P(None, "gz"),) * 3 + (P(None, "gz", None),),
        out_specs=field,
        check_vma=False,
    )
```

```python
import functools

import jax
import jax.numpy as jnp
from jax import lax
from jax.experimental import pallas as pl
from jax.experimental.pallas import tpu as pltpu
from jax.sharding import PartitionSpec as P

MESH = pl.DeviceIdType.MESH
LANES = 128
SUB = 8
WIN = 16
HMAX = 8
KB = 4096
NK = 16
F32 = jnp.float32
BF16 = jnp.bfloat16


def load_rows(ref, p, b, steps):
    return ref[p, pl.ds(b, SUB, stride=steps), :]


def step_loop(count, unroll, body, init):
    def outer(i, carry):
        for j in range(unroll):
            carry = body(i * unroll + j, carry)
        return carry

    return lax.fori_loop(0, count // unroll, outer, init)


def network(is_top, u_ref, win_ref, w_in_ref, vec_ref, w_mid_ref, cols_ref, wl_ref, samp_ref, table_ref):
    planes, levels, _ = u_ref.shape
    vectors = jnp.concatenate(
        [w_in_ref[...], vec_ref[0], vec_ref[1], vec_ref[2], jnp.zeros((2, LANES), F32)], axis=0
    )
    columns = vectors.T
    for c in range(6):
        cols_ref[c] = jnp.broadcast_to(columns[:, c : c + 1], (LANES, LANES))
    mid = w_mid_ref[...].T
    mid_hi = mid.astype(BF16)
    mid_lo = (mid - mid_hi.astype(F32)).astype(BF16)
    wl_ref[...] = jnp.concatenate(
        [jnp.concatenate([mid_hi, mid_hi], axis=1), jnp.concatenate([mid_lo, mid_lo], axis=1)], axis=0
    )
    for p in range(planes):
        samp_ref[0, p * HMAX : (p + 1) * HMAX, :] = jnp.where(
            is_top, u_ref[p, levels - 1 - HMAX : levels - 1, :], u_ref[p, 1 : 1 + HMAX, :]
        )
        for c in range(2):
            samp_ref[1 + c, p * HMAX : (p + 1) * HMAX, :] = jnp.where(
                is_top, win_ref[c, p, WIN - 1 - HMAX : WIN - 1, :], win_ref[c, p, 1 : 1 + HMAX, :]
            )

    @pl.loop(0, planes * HMAX // NK)
    def _(i):
        halves = []
        for h in range(NK):
            k = i * NK + h
            pre = cols_ref[3]
            for c in range(3):
                pre = pre + cols_ref[c] * samp_ref[c, pl.ds(k, 1), :]
            hidden = jnp.tanh(pre)
            upper = hidden.astype(BF16)
            lower = (hidden - upper.astype(F32)).astype(BF16)
            halves.append(jnp.concatenate([upper, lower], axis=0))
        mixed = jnp.dot(wl_ref[...], jnp.concatenate(halves, axis=1), preferred_element_type=F32)
        for h in range(NK):
            part = mixed[:, h * LANES : (h + 1) * LANES]
            second = jnp.tanh(part[:LANES] + part[LANES:] + cols_ref[4])
            table_ref[pl.ds(i * NK + h, 1), :] = jnp.sum(second * cols_ref[5], axis=0, keepdims=True)


def binning(is_top, nx, nyc, cell_ref, height_ref, face_ref, owner_ref, table_ref, acc_ref):
    rows = cell_ref.shape[1]
    planes = table_ref.shape[0] // HMAX
    acc_ref[...] = jnp.zeros_like(acc_ref)
    bins = acc_ref.shape[0]
    row = lax.broadcasted_iota(jnp.int32, (SUB, LANES), 0)
    rows_iota = lax.broadcasted_iota(jnp.int32, (LANES, KB), 0)
    bins_iota = lax.broadcasted_iota(jnp.int32, (bins, KB), 0)

    @pl.loop(0, rows // KB)
    def _(i):
        at = pl.ds(pl.multiple_of(i * KB, KB), KB)

        def wall(ref):
            return jnp.where(is_top, ref[1:2, at], ref[0:1, at])

        cell, height, face = wall(cell_ref), wall(height_ref), wall(face_ref)
        owner = owner_ref[:, pl.ds(pl.multiple_of(jnp.where(is_top, rows, 0) + i * KB, KB), KB)]
        span = cell % LANES
        key = (cell // LANES) * HMAX + jnp.where(is_top, HMAX - height, height - 1)
        picks = []
        for j in range(KB // LANES):
            cut = slice(j * LANES, (j + 1) * LANES)
            index = jnp.broadcast_to(span[:, cut], (SUB, LANES))
            keyed = jnp.broadcast_to(key[:, cut], (SUB, LANES))
            value = jnp.zeros((SUB, LANES), F32)
            for t in range(planes):
                got = jnp.take_along_axis(table_ref[t * HMAX : (t + 1) * HMAX, :], index, axis=1)
                value = value + jnp.where(keyed == row + t * HMAX, got, 0.0)
            picks.append(jnp.sum(value, axis=0, keepdims=True))
        value = jnp.concatenate(picks, axis=1)
        first = value.astype(BF16).astype(F32)
        rest = value - first
        low = face % LANES
        high = (owner % nyc) * (2 * nx) + (owner // nyc) * 2 + face // LANES
        onto = jnp.where(bins_iota == high, 1.0, 0.0).astype(BF16)
        named = rows_iota == low
        carried = jnp.concatenate(
            [jnp.where(named, first, 0.0).astype(BF16), jnp.where(named, rest, 0.0).astype(BF16)], axis=0
        )
        acc_ref[...] += lax.dot_general(
            onto, carried, (((1,), (1,)), ((), ())), preferred_element_type=F32
        )


def kernel(
    gz,
    gy,
    nx,
    u_hbm,
    v_hbm,
    w_hbm,
    s_hbm,
    w_in_hbm,
    b_in_hbm,
    w_mid_hbm,
    b_mid_hbm,
    w_out_hbm,
    cell_hbm,
    height_hbm,
    face_hbm,
    owner_hbm,
    out_ref,
    u_ref,
    s_ref,
    win_ref,
    w_in_ref,
    vec_ref,
    w_mid_ref,
    cell_ref,
    height_ref,
    face_ref,
    owner_ref,
    cols_ref,
    wl_ref,
    samp_ref,
    table_ref,
    acc_ref,
    keep_ref,
    gain_ref,
    gsrc_ref,
    lf_ref,
    ff_ref,
    bl_ref,
    q_ref,
    fb_ref,
    pack_ref,
    halo_ref,
    send_a,
    recv_a,
    send_b,
    recv_b,
    send_s,
    recv_s,
    load_sem,
    halo_send,
    halo_recv,
    a_send,
    a_recv,
    b_send,
    b_recv,
    s_send,
    s_recv,
):
    planes, levels, _ = u_ref.shape
    steps = levels // SUB
    total_steps = planes * steps
    nyc = gz // nx
    roles = (0, 1, gy - 2, gy - 1)
    me = lax.axis_index("gz")
    level = lax.axis_index("gy")
    xx = me // nyc
    yc = me % nyc
    is_top = level >= gy // 2
    is_tot = (level == 0) | (level == gy - 1)
    is_role = is_tot | (level == 1) | (level == gy - 2)
    role = jnp.where(is_top, level - (gy - 4), level)

    start = pl.multiple_of(jnp.where(is_top, levels - WIN, 0), 8)
    load_u = pltpu.make_async_copy(u_hbm, u_ref, load_sem.at[0])
    load_s = pltpu.make_async_copy(s_hbm, s_ref, load_sem.at[1])
    lists = [
        pltpu.make_async_copy(src, dst, load_sem.at[2 + i])
        for i, (src, dst) in enumerate(
            [(cell_hbm, cell_ref), (height_hbm, height_ref), (face_hbm, face_ref), (owner_hbm, owner_ref)]
        )
    ]
    weights = [
        pltpu.make_async_copy(src, dst, load_sem.at[6 + i])
        for i, (src, dst) in enumerate(
            [
                (w_in_hbm, w_in_ref),
                (b_in_hbm, vec_ref.at[0]),
                (b_mid_hbm, vec_ref.at[1]),
                (w_out_hbm, vec_ref.at[2]),
                (w_mid_hbm, w_mid_ref),
                (v_hbm.at[:, pl.ds(start, WIN), :], win_ref.at[0]),
                (w_hbm.at[:, pl.ds(start, WIN), :], win_ref.at[1]),
            ]
        )
    ]
    load_u.start()

    @pl.when(is_tot)
    def _():
        for copy in weights:
            copy.start()

    @pl.when(is_role)
    def _():
        for copy in lists:
            copy.start()

    load_s.start()

    barrier = pltpu.get_barrier_semaphore()

    def greet(z, y):
        pl.semaphore_signal(barrier, inc=1, device_id=(z, y), device_id_type=MESH)

    left, right = lax.rem(me + gz - 1, gz), lax.rem(me + 1, gz)
    greet(left, level)
    greet(right, level)

    @pl.loop(1, gy)
    def _(d):
        greet(me, lax.rem(level + d, gy))

    @pl.loop(1, nx)
    def _(d):
        for r in roles:
            greet(lax.rem(xx + d, nx) * nyc + yc, r)

    @pl.when(is_role)
    def _():
        @pl.loop(1, nyc)
        def _(d):
            greet(xx * nyc + lax.rem(yc + d, nyc), level)

    lane = lax.broadcasted_iota(jnp.int32, (SUB, LANES), 1)
    row = lax.broadcasted_iota(jnp.int32, (SUB, LANES), 0)
    load_u.wait()
    packed = jnp.zeros((SUB, LANES), F32)
    for p in range(planes):

        def pack(b, acc, p=p):
            i = p * steps + b
            return jnp.where(lane // 2 == i, pltpu.roll(load_rows(u_ref, p, b, steps), 2 * i + 1, 1), acc)

        packed = step_loop(steps, 8, pack, packed)
    pack_ref[...] = packed

    base = gy - 1 + 2

    @pl.when(is_role)
    def _():
        pl.semaphore_wait(barrier, base + nyc - 1 + (nx - 1) * gy)

    @pl.when(jnp.logical_not(is_role))
    def _():
        pl.semaphore_wait(barrier, base)

    halo_copies = [
        pltpu.make_async_remote_copy(
            src_ref=pack_ref,
            dst_ref=halo_ref.at[slot],
            send_sem=halo_send.at[slot],
            recv_sem=halo_recv.at[slot],
            device_id=(z, level),
            device_id_type=MESH,
        )
        for slot, z in ((0, right), (1, left))
    ]
    for copy in halo_copies:
        copy.start()

    def copy_a(z, slot):
        return pltpu.make_async_remote_copy(
            src_ref=send_a.at[z],
            dst_ref=recv_a.at[slot],
            send_sem=a_send,
            recv_sem=a_recv,
            device_id=(xx * nyc + z, level),
            device_id_type=MESH,
        )

    def copy_b(x, y):
        return pltpu.make_async_remote_copy(
            src_ref=send_b.at[x],
            dst_ref=recv_b.at[role * nx + xx],
            send_sem=b_send,
            recv_sem=b_recv,
            device_id=(x * nyc + yc, y),
            device_id_type=MESH,
        )

    def copy_s(y):
        return pltpu.make_async_remote_copy(
            src_ref=send_s,
            dst_ref=recv_s.at[level],
            send_sem=s_send,
            recv_sem=s_recv,
            device_id=(me, y),
            device_id_type=MESH,
        )

    @pl.when(is_tot)
    def _():
        for copy in weights:
            copy.wait()
        network(is_top, u_ref, win_ref, w_in_ref, vec_ref, w_mid_ref, cols_ref, wl_ref, samp_ref, table_ref)

    @pl.when(is_role & jnp.logical_not(is_tot))
    def _():
        table_ref[...] = jnp.ones_like(table_ref)

    @pl.when(is_role)
    def _():
        for copy in lists:
            copy.wait()
        binning(is_top, nx, nyc, cell_ref, height_ref, face_ref, owner_ref, table_ref, acc_ref)
        binned = acc_ref[:, :LANES] + acc_ref[:, LANES:]
        send_a[...] = binned.reshape(send_a.shape)
        recv_a[yc] = send_a[yc]

        for d in sorted(range(1, nyc), key=lambda d: -min(d, nyc - d)):
            copy_a(lax.rem(yc + d, nyc), yc).start()

    load_s.wait()
    for copy in halo_copies:
        copy.wait_recv()
    merged = jnp.where(lane % 2 == 1, pltpu.roll(halo_ref[0], 1, 1), pltpu.roll(halo_ref[1], LANES - 1, 1))
    zero, one = jnp.zeros((SUB, LANES), F32), jnp.ones((SUB, LANES), F32)
    summaries = []
    for p in range(planes):

        def prepare(b, _, p=p):
            i = p * steps + b
            stiff = load_rows(s_ref, p, b, steps)
            here = load_rows(u_ref, p, b, steps)
            halo = pltpu.roll(merged, LANES - 1 - 2 * i, 1)
            before = jnp.where(lane == 0, halo, pltpu.roll(here, 1, 1))
            after = jnp.where(lane == LANES - 1, halo, pltpu.roll(here, LANES - 1, 1))
            source = here + 0.2 * (after + before - 2.0 * here)
            gain = 1.0 / (1.0 + stiff)
            keep_ref[p, b] = stiff * gain
            gain_ref[p, b] = gain
            gsrc_ref[p, b] = gain * source
            return _

        step_loop(steps, 4, prepare, 0)

    def forward(b, carry):
        out = []
        for p in range(planes):
            value, factor = carry[2 * p : 2 * p + 2]
            keep = keep_ref[p, b]
            value = keep * value + gsrc_ref[p, b]
            factor = keep * factor
            lf_ref[p, b] = value
            ff_ref[p, b] = factor
            out += [value, factor]
        return tuple(out)

    forwards = step_loop(steps, 4, forward, (zero, one) * planes)

    def backward(t, carry):
        out = []
        b = steps - 1 - t
        for p in range(planes):
            value, response, factor = carry[3 * p : 3 * p + 3]
            keep, gain = keep_ref[p, b], gain_ref[p, b]
            value = keep * value + gain * lf_ref[p, b]
            response = keep * response + gain * ff_ref[p, b]
            factor = keep * factor
            bl_ref[p, b] = value
            q_ref[p, b] = response
            fb_ref[p, b] = factor
            out += [value, response, factor]
        return tuple(out)

    backwards = step_loop(steps, 4, backward, (zero, zero, one) * planes)

    inner = []
    for p in range(planes):
        local_f = forwards[2 * p]
        local_b, response, product = backwards[3 * p : 3 * p + 3]
        pi, li = product, local_f
        for d in (1, 2, 4):
            ok = row >= d
            lp = jnp.where(ok, pltpu.roll(li, d, 0), 0.0)
            pp = jnp.where(ok, pltpu.roll(pi, d, 0), 1.0)
            li, pi = pi * lp + li, pi * pp
        pf = jnp.where(row >= 1, pltpu.roll(pi, 1, 0), 1.0)
        lf = jnp.where(row >= 1, pltpu.roll(li, 1, 0), 0.0)
        pb, cb, qb = product, local_b + response * lf, response * pf
        for d in (1, 2, 4):
            ok = row < SUB - d
            cp = jnp.where(ok, pltpu.roll(cb, SUB - d, 0), 0.0)
            qp = jnp.where(ok, pltpu.roll(qb, SUB - d, 0), 0.0)
            pp = jnp.where(ok, pltpu.roll(pb, SUB - d, 0), 1.0)
            cb, qb, pb = pb * cp + cb, pb * qp + qb, pb * pp
        ok = row < SUB - 1
        summaries.append((pb[0:1], li[SUB - 1 : SUB], cb[0:1], qb[0:1]))
        inner.append(
            (
                pf,
                lf,
                jnp.where(ok, pltpu.roll(pb, SUB - 1, 0), 1.0),
                jnp.where(ok, pltpu.roll(cb, SUB - 1, 0), 0.0),
                jnp.where(ok, pltpu.roll(qb, SUB - 1, 0), 0.0),
            )
        )
    own_alpha = jnp.concatenate([1.0 / keep_ref[p, 0, 0:1] for p in range(planes)], axis=0)
    own_eps = jnp.concatenate([1.0 / s_ref[p, levels - 1 : levels, :] for p in range(planes)], axis=0)
    at_bottom, at_top = level == 0, level == gy - 1
    blocks = [jnp.concatenate([summaries[p][c] for p in range(planes)], axis=0) for c in range(4)]
    blocks[0] = blocks[0] * jnp.where(at_bottom, own_alpha, jnp.where(at_top, own_eps, 1.0))
    summary = jnp.concatenate(blocks, axis=0)
    send_s[...] = summary
    recv_s[level] = summary

    @pl.loop(1, gy)
    def _(d):
        copy_s(lax.rem(level + d, gy)).start()

    @pl.when(is_role)
    def _():
        pltpu.make_async_copy(recv_a.at[pl.ds(0, nyc - 1)], recv_a.at[pl.ds(0, nyc - 1)], a_recv).wait()
        part = recv_a[0]
        for i in range(1, nyc):
            part = part + recv_a[i]
        for x in range(nx):
            send_b[x] = part[2 * x : 2 * x + 2, :]
        recv_b[role * nx + xx] = send_b[xx]

        for y in range(gy):
            for d in sorted(range(1, nx), key=lambda d: -min(d, nx - d)):
                copy_b(lax.rem(xx + d, nx), y).start()

            @pl.when(level != y)
            def _(y=y):
                copy_b(xx, y).start()

    pltpu.make_async_copy(recv_s.at[pl.ds(0, gy - 1)], recv_s.at[pl.ds(0, gy - 1)], s_recv).wait()

    def block(g, c):
        return recv_s[g, 2 * c : 2 * c + 2, :]

    alphas, betas = [None, block(0, 0)], [None, block(0, 1)]
    for g in range(1, gy - 1):
        alphas.append(block(g, 0) * alphas[g])
        betas.append(block(g, 0) * betas[g] + block(g, 1))
    alpha, beta = jnp.where(at_bottom, own_alpha, 0.0), jnp.zeros_like(own_alpha)
    for g in range(1, gy):
        alpha = jnp.where(level == g, alphas[g], alpha)
        beta = jnp.where(level == g, betas[g], beta)
    top = gy - 1
    gam, dlt, eps = block(top, 3) * alphas[top], block(top, 2) + block(top, 3) * betas[top], block(top, 0)
    gamma, delta = jnp.zeros_like(own_alpha), jnp.zeros_like(own_alpha)
    epsilon = jnp.where(at_top, own_eps, 0.0)
    for g in range(gy - 2, -1, -1):
        gamma = jnp.where(level == g, gam, gamma)
        delta = jnp.where(level == g, dlt, delta)
        epsilon = jnp.where(level == g, eps, epsilon)
        if g:
            gam = block(g, 0) * gam + block(g, 3) * alphas[g]
            dlt = block(g, 0) * dlt + block(g, 2) + block(g, 3) * betas[g]
            eps = block(g, 0) * eps

    count = 4 * nx

    @pl.when(is_role)
    def _():
        pltpu.make_async_copy(recv_b.at[pl.ds(0, count - 1)], recv_b.at[pl.ds(0, count - 1)], b_recv).wait()

    @pl.when(jnp.logical_not(is_role))
    def _():
        pltpu.make_async_copy(recv_b, recv_b, b_recv).wait()

    sums = []
    for r in range(4):
        total = recv_b[r * nx]
        for x in range(1, nx):
            total = total + recv_b[r * nx + x]
        sums.append(total)
    stress_low = sums[0] / jnp.maximum(sums[1], 1.0)
    stress_top = sums[3] / jnp.maximum(sums[2], 1.0)
    f_in = alpha * stress_low + beta
    b_in = gamma * stress_low + delta + epsilon * stress_top
    for p in range(planes):
        pf, lf, pb, cb, qb = inner[p]
        below = pf * f_in[p : p + 1] + lf
        above = pb * b_in[p : p + 1] + cb + qb * f_in[p : p + 1]

        def finish(b, _, p=p, below=below, above=above):
            out_ref[p, pl.ds(b, SUB, stride=steps), :] = bl_ref[p, b] + q_ref[p, b] * below + fb_ref[p, b] * above
            return _

        step_loop(steps, steps, finish, 0)

    for copy in halo_copies:
        copy.wait_send()
    pltpu.make_async_copy(recv_s.at[pl.ds(0, gy - 1)], recv_s.at[pl.ds(0, gy - 1)], s_send).wait()

    @pl.when(is_role)
    def _():
        pltpu.make_async_copy(send_a.at[pl.ds(0, nyc - 1)], send_a.at[pl.ds(0, nyc - 1)], a_send).wait()
        for _ in range(gy - 1):
            pltpu.make_async_copy(send_b, send_b, b_send).wait()
        pltpu.make_async_copy(send_b.at[pl.ds(0, nx - 1)], send_b.at[pl.ds(0, nx - 1)], b_send).wait()


def local(gz, gy, nx, *args):
    u, v, w, s, w_in, b_in, w_mid, b_mid, w_out, cell, height, face, owner = args
    planes, levels, span = u.shape
    steps = levels // SUB
    nyc = gz // nx
    rows = cell.shape[1]
    vmem = pltpu.VMEM
    scratch = [
        vmem(u.shape, F32),
        vmem(u.shape, F32),
        vmem((2, planes, WIN, span), F32),
        vmem((3, span), F32),
        vmem((3, 1, span), F32),
        vmem((span, span), F32),
        vmem((2, rows), jnp.int32),
        vmem((2, rows), jnp.int32),
        vmem((2, rows), jnp.int32),
        vmem((1, 2 * rows), jnp.int32),
        vmem((6, span, span), F32),
        vmem((2 * span, 2 * span), BF16),
        vmem((3, planes * HMAX, span), F32),
        vmem((planes * HMAX, span), F32),
        vmem((2 * gz, 2 * span), F32),
        vmem((planes, steps, SUB, span), F32),
        vmem((planes, steps, SUB, span), F32),
        vmem((planes, steps, SUB, span), F32),
        vmem((planes, steps, SUB, span), F32),
        vmem((planes, steps, SUB, span), F32),
        vmem((planes, steps, SUB, span), F32),
        vmem((planes, steps, SUB, span), F32),
        vmem((planes, steps, SUB, span), F32),
        vmem((SUB, span), F32),
        vmem((2, SUB, span), F32),
        vmem((nyc, 2 * nx, span), F32),
        vmem((nyc, 2 * nx, span), F32),
        vmem((nx, 2, span), F32),
        vmem((4 * nx, 2, span), F32),
        vmem((8, span), F32),
        vmem((gy, 8, span), F32),
        pltpu.SemaphoreType.DMA((13,)),
        pltpu.SemaphoreType.DMA((2,)),
        pltpu.SemaphoreType.DMA((2,)),
    ] + [pltpu.SemaphoreType.DMA] * 6
    operands = [
        u,
        v,
        w,
        s,
        w_in,
        b_in[None, :],
        w_mid,
        b_mid[None, :],
        w_out[None, :],
        cell,
        height,
        face,
        owner.reshape(1, 2 * rows),
    ]
    return pl.pallas_call(
        functools.partial(kernel, gz, gy, nx),
        out_shape=jax.ShapeDtypeStruct(u.shape, F32),
        in_specs=[pl.BlockSpec(memory_space=pl.ANY)] * 13,
        out_specs=pl.BlockSpec(memory_space=pltpu.VMEM),
        scratch_shapes=scratch,
        compiler_params=pltpu.CompilerParams(
            collective_id=0, has_side_effects=True, vmem_limit_bytes=40 * 2**20
        ),
    )(*[pltpu.with_memory_space_constraint(x, pltpu.HBM) for x in operands])


def solution(mesh):
    field = P(None, "gy", "gz")
    gz, gy = mesh.shape["gz"], mesh.shape["gy"]
    return jax.shard_map(
        functools.partial(local, gz, gy, 4),
        mesh=mesh,
        in_specs=(field,) * 4 + (P(),) * 5 + (P(None, "gz"),) * 3 + (P(None, "gz", None),),
        out_specs=field,
        check_vma=False,
    )
```

```python
import functools

import jax
import jax.numpy as jnp
from jax import lax
from jax.experimental import pallas as pl
from jax.experimental.pallas import tpu as pltpu
from jax.sharding import PartitionSpec as P

MESH = pl.DeviceIdType.MESH
LANES = 128
SUB = 8
WIN = 16
HMAX = 8
KB = 4096
NK = 16
F32 = jnp.float32
BF16 = jnp.bfloat16


def load_rows(ref, p, b, steps):
    return ref[p, pl.ds(b, SUB, stride=steps), :]


def step_loop(count, unroll, body, init):
    def outer(i, carry):
        for j in range(unroll):
            carry = body(i * unroll + j, carry)
        return carry

    return lax.fori_loop(0, count // unroll, outer, init)


def network(is_top, u_ref, win_ref, w_in_ref, vec_ref, w_mid_ref, cols_ref, wl_ref, samp_ref, table_ref):
    planes, levels, _ = u_ref.shape
    vectors = jnp.concatenate(
        [w_in_ref[...], vec_ref[0], vec_ref[1], vec_ref[2], jnp.zeros((2, LANES), F32)], axis=0
    )
    columns = vectors.T
    for c in range(6):
        cols_ref[c] = jnp.broadcast_to(columns[:, c : c + 1], (LANES, LANES))
    mid = w_mid_ref[...].T
    mid_hi = mid.astype(BF16)
    mid_lo = (mid - mid_hi.astype(F32)).astype(BF16)
    wl_ref[...] = jnp.concatenate(
        [jnp.concatenate([mid_hi, mid_hi], axis=1), jnp.concatenate([mid_lo, mid_lo], axis=1)], axis=0
    )
    for p in range(planes):
        samp_ref[0, p * HMAX : (p + 1) * HMAX, :] = jnp.where(
            is_top, u_ref[p, levels - 1 - HMAX : levels - 1, :], u_ref[p, 1 : 1 + HMAX, :]
        )
        for c in range(2):
            samp_ref[1 + c, p * HMAX : (p + 1) * HMAX, :] = jnp.where(
                is_top, win_ref[c, p, WIN - 1 - HMAX : WIN - 1, :], win_ref[c, p, 1 : 1 + HMAX, :]
            )

    @pl.loop(0, planes * HMAX // NK)
    def _(i):
        halves = []
        for h in range(NK):
            k = i * NK + h
            pre = cols_ref[3]
            for c in range(3):
                pre = pre + cols_ref[c] * samp_ref[c, pl.ds(k, 1), :]
            hidden = jnp.tanh(pre)
            upper = hidden.astype(BF16)
            lower = (hidden - upper.astype(F32)).astype(BF16)
            halves.append(jnp.concatenate([upper, lower], axis=0))
        mixed = jnp.dot(wl_ref[...], jnp.concatenate(halves, axis=1), preferred_element_type=F32)
        for h in range(NK):
            part = mixed[:, h * LANES : (h + 1) * LANES]
            second = jnp.tanh(part[:LANES] + part[LANES:] + cols_ref[4])
            table_ref[pl.ds(i * NK + h, 1), :] = jnp.sum(second * cols_ref[5], axis=0, keepdims=True)


def binning(is_top, nx, nyc, cell_ref, height_ref, face_ref, owner_ref, table_ref, acc_ref):
    rows = cell_ref.shape[1]
    planes = table_ref.shape[0] // HMAX
    acc_ref[...] = jnp.zeros_like(acc_ref)
    bins = acc_ref.shape[0]
    row = lax.broadcasted_iota(jnp.int32, (SUB, LANES), 0)
    rows_iota = lax.broadcasted_iota(jnp.int32, (LANES, KB), 0)
    bins_iota = lax.broadcasted_iota(jnp.int32, (bins, KB), 0)

    @pl.loop(0, rows // KB)
    def _(i):
        at = pl.ds(pl.multiple_of(i * KB, KB), KB)

        def wall(ref):
            return jnp.where(is_top, ref[1:2, at], ref[0:1, at])

        cell, height, face = wall(cell_ref), wall(height_ref), wall(face_ref)
        owner = owner_ref[:, pl.ds(pl.multiple_of(jnp.where(is_top, rows, 0) + i * KB, KB), KB)]
        span = cell % LANES
        key = (cell // LANES) * HMAX + jnp.where(is_top, HMAX - height, height - 1)
        picks = []
        for j in range(KB // LANES):
            cut = slice(j * LANES, (j + 1) * LANES)
            index = jnp.broadcast_to(span[:, cut], (SUB, LANES))
            keyed = jnp.broadcast_to(key[:, cut], (SUB, LANES))
            value = jnp.zeros((SUB, LANES), F32)
            for t in range(planes):
                got = jnp.take_along_axis(table_ref[t * HMAX : (t + 1) * HMAX, :], index, axis=1)
                value = value + jnp.where(keyed == row + t * HMAX, got, 0.0)
            picks.append(jnp.sum(value, axis=0, keepdims=True))
        value = jnp.concatenate(picks, axis=1)
        first = value.astype(BF16).astype(F32)
        rest = value - first
        low = face % LANES
        high = (owner % nyc) * (2 * nx) + (owner // nyc) * 2 + face // LANES
        onto = jnp.where(bins_iota == high, 1.0, 0.0).astype(BF16)
        named = rows_iota == low
        carried = jnp.concatenate(
            [jnp.where(named, first, 0.0).astype(BF16), jnp.where(named, rest, 0.0).astype(BF16)], axis=0
        )
        acc_ref[...] += lax.dot_general(
            onto, carried, (((1,), (1,)), ((), ())), preferred_element_type=F32
        )


def kernel(
    gz,
    gy,
    nx,
    u_hbm,
    v_hbm,
    w_hbm,
    s_hbm,
    w_in_hbm,
    b_in_hbm,
    w_mid_hbm,
    b_mid_hbm,
    w_out_hbm,
    cell_hbm,
    height_hbm,
    face_hbm,
    owner_hbm,
    out_ref,
    u_ref,
    s_ref,
    win_ref,
    w_in_ref,
    vec_ref,
    w_mid_ref,
    cell_ref,
    height_ref,
    face_ref,
    owner_ref,
    cols_ref,
    wl_ref,
    samp_ref,
    table_ref,
    acc_ref,
    keep_ref,
    gain_ref,
    gsrc_ref,
    lf_ref,
    ff_ref,
    bl_ref,
    q_ref,
    fb_ref,
    pack_ref,
    halo_ref,
    send_a,
    recv_a,
    send_b,
    recv_b,
    send_d,
    recv_d,
    high_ref,
    send_s,
    recv_s,
    load_sem,
    halo_send,
    halo_recv,
    a_send,
    a_recv,
    b_send,
    b_recv,
    d_send,
    d_recv,
    s_send,
    s_recv,
):
    planes, levels, _ = u_ref.shape
    steps = levels // SUB
    total_steps = planes * steps
    nyc = gz // nx
    me = lax.axis_index("gz")
    level = lax.axis_index("gy")
    xx = me // nyc
    yc = me % nyc
    is_low, is_high = level == 0, level == gy - 1
    is_top = (level == 1) | is_high
    is_tot = is_low | is_high
    is_role = (level <= 2) | is_high
    role = jnp.where(is_high, 3, level)
    roles = (0, 1, 2, gy - 1)

    start = pl.multiple_of(jnp.where(is_top, levels - WIN, 0), 8)
    load_u = pltpu.make_async_copy(u_hbm, u_ref, load_sem.at[0])
    load_s = pltpu.make_async_copy(s_hbm, s_ref, load_sem.at[1])
    lists = [
        pltpu.make_async_copy(src, dst, load_sem.at[2 + i])
        for i, (src, dst) in enumerate(
            [(cell_hbm, cell_ref), (height_hbm, height_ref), (face_hbm, face_ref), (owner_hbm, owner_ref)]
        )
    ]
    weights = [
        pltpu.make_async_copy(src, dst, load_sem.at[6 + i])
        for i, (src, dst) in enumerate(
            [
                (w_in_hbm, w_in_ref),
                (b_in_hbm, vec_ref.at[0]),
                (b_mid_hbm, vec_ref.at[1]),
                (w_out_hbm, vec_ref.at[2]),
                (w_mid_hbm, w_mid_ref),
                (v_hbm.at[:, pl.ds(start, WIN), :], win_ref.at[0]),
                (w_hbm.at[:, pl.ds(start, WIN), :], win_ref.at[1]),
            ]
        )
    ]
    load_u.start()

    @pl.when(is_tot)
    def _():
        for copy in weights:
            copy.start()

    @pl.when(is_role)
    def _():
        for copy in lists:
            copy.start()

    load_s.start()

    barrier = pltpu.get_barrier_semaphore()

    def greet(z, y):
        pl.semaphore_signal(barrier, inc=1, device_id=(z, y), device_id_type=MESH)

    left, right = lax.rem(me + gz - 1, gz), lax.rem(me + 1, gz)
    greet(left, level)
    greet(right, level)

    @pl.loop(1, gy)
    def _(d):
        greet(me, lax.rem(level + d, gy))

    @pl.loop(1, nx)
    def _(d):
        for y in roles[:-1]:
            greet(lax.rem(xx + d, nx) * nyc + yc, y)

    @pl.when(is_low)
    def _():
        @pl.loop(1, gz)
        def _(d):
            greet(lax.rem(me + d, gz), gy - 1)

    @pl.when(jnp.logical_not(is_low))
    def _():
        @pl.loop(1, nx)
        def _(d):
            greet(lax.rem(xx + d, nx) * nyc + yc, gy - 1)

    @pl.when(is_role)
    def _():
        @pl.loop(1, nyc)
        def _(d):
            greet(xx * nyc + lax.rem(yc + d, nyc), level)

    lane = lax.broadcasted_iota(jnp.int32, (SUB, LANES), 1)
    row = lax.broadcasted_iota(jnp.int32, (SUB, LANES), 0)
    load_u.wait()
    packed = jnp.zeros((SUB, LANES), F32)
    for p in range(planes):

        def pack(b, acc, p=p):
            i = p * steps + b
            return jnp.where(lane // 2 == i, pltpu.roll(load_rows(u_ref, p, b, steps), 2 * i + 1, 1), acc)

        packed = step_loop(steps, 8, pack, packed)
    pack_ref[...] = packed

    @pl.when(is_tot)
    def _():
        for copy in weights:
            copy.wait()
        network(is_top, u_ref, win_ref, w_in_ref, vec_ref, w_mid_ref, cols_ref, wl_ref, samp_ref, table_ref)

    @pl.when(is_role & jnp.logical_not(is_tot))
    def _():
        table_ref[...] = jnp.ones_like(table_ref)

    @pl.when(is_role)
    def _():
        for copy in lists:
            copy.wait()
        binning(is_top, nx, nyc, cell_ref, height_ref, face_ref, owner_ref, table_ref, acc_ref)

    base = gy - 1 + 2

    @pl.when(is_role & jnp.logical_not(is_high))
    def _():
        pl.semaphore_wait(barrier, base + nyc - 1 + (nx - 1) * gy)

    @pl.when(is_high)
    def _():
        pl.semaphore_wait(barrier, base + nyc - 1 + (nx - 1) * (gy - 1) + gz - 1)

    @pl.when(jnp.logical_not(is_role))
    def _():
        pl.semaphore_wait(barrier, base)

    halo_copies = [
        pltpu.make_async_remote_copy(
            src_ref=pack_ref,
            dst_ref=halo_ref.at[slot],
            send_sem=halo_send.at[slot],
            recv_sem=halo_recv.at[slot],
            device_id=(z, level),
            device_id_type=MESH,
        )
        for slot, z in ((0, right), (1, left))
    ]
    for copy in halo_copies:
        copy.start()

    def copy_a(z, slot):
        return pltpu.make_async_remote_copy(
            src_ref=send_a.at[z],
            dst_ref=recv_a.at[slot],
            send_sem=a_send,
            recv_sem=a_recv,
            device_id=(xx * nyc + z, level),
            device_id_type=MESH,
        )

    def copy_b(x, y):
        return pltpu.make_async_remote_copy(
            src_ref=send_b.at[x],
            dst_ref=recv_b.at[role * nx + xx],
            send_sem=b_send,
            recv_sem=b_recv,
            device_id=(x * nyc + yc, y),
            device_id_type=MESH,
        )

    def copy_d(x, z):
        return pltpu.make_async_remote_copy(
            src_ref=send_d.at[z * nx + x],
            dst_ref=recv_d.at[me],
            send_sem=d_send,
            recv_sem=d_recv,
            device_id=(x * nyc + z, 0),
            device_id_type=MESH,
        )

    def copy_s(y):
        return pltpu.make_async_remote_copy(
            src_ref=send_s,
            dst_ref=recv_s.at[level],
            send_sem=s_send,
            recv_sem=s_recv,
            device_id=(me, y),
            device_id_type=MESH,
        )

    @pl.when(is_role)
    def _():
        binned = acc_ref[:, :LANES] + acc_ref[:, LANES:]

        send_a[...] = binned.reshape(send_a.shape)
        recv_a[yc] = send_a[yc]
        for d in sorted(range(1, nyc), key=lambda d: -min(d, nyc - d)):
            copy_a(lax.rem(yc + d, nyc), yc).start()

    @pl.when(is_high)
    def _():
        send_d[...] = (acc_ref[:, :LANES] + acc_ref[:, LANES:]).reshape(send_d.shape)
        for dx in sorted(range(nx), key=lambda d: -min(d, nx - d)):

            @pl.loop(0, nyc)
            def _(t, dx=dx):
                away = (t + 1) // 2
                dz = jnp.where(t % 2 == 1, nyc // 2 + away, nyc // 2 - away + nyc)
                copy_d(lax.rem(xx + dx, nx), lax.rem(yc + dz, nyc)).start()

    load_s.wait()
    for copy in halo_copies:
        copy.wait_recv()
    merged = jnp.where(lane % 2 == 1, pltpu.roll(halo_ref[0], 1, 1), pltpu.roll(halo_ref[1], LANES - 1, 1))
    zero, one = jnp.zeros((SUB, LANES), F32), jnp.ones((SUB, LANES), F32)
    summaries = []
    for p in range(planes):

        def prepare(b, _, p=p):
            i = p * steps + b
            stiff = load_rows(s_ref, p, b, steps)
            here = load_rows(u_ref, p, b, steps)
            halo = pltpu.roll(merged, LANES - 1 - 2 * i, 1)
            before = jnp.where(lane == 0, halo, pltpu.roll(here, 1, 1))
            after = jnp.where(lane == LANES - 1, halo, pltpu.roll(here, LANES - 1, 1))
            source = here + 0.2 * (after + before - 2.0 * here)
            gain = 1.0 / (1.0 + stiff)
            keep_ref[p, b] = stiff * gain
            gain_ref[p, b] = gain
            gsrc_ref[p, b] = gain * source
            return _

        step_loop(steps, 4, prepare, 0)

    def forward(b, carry):
        out = []
        for p in range(planes):
            value, factor = carry[2 * p : 2 * p + 2]
            keep = keep_ref[p, b]
            value = keep * value + gsrc_ref[p, b]
            factor = keep * factor
            lf_ref[p, b] = value
            ff_ref[p, b] = factor
            out += [value, factor]
        return tuple(out)

    forwards = step_loop(steps, 4, forward, (zero, one) * planes)

    def backward(t, carry):
        out = []
        b = steps - 1 - t
        for p in range(planes):
            value, response, factor = carry[3 * p : 3 * p + 3]
            keep, gain = keep_ref[p, b], gain_ref[p, b]
            value = keep * value + gain * lf_ref[p, b]
            response = keep * response + gain * ff_ref[p, b]
            factor = keep * factor
            bl_ref[p, b] = value
            q_ref[p, b] = response
            fb_ref[p, b] = factor
            out += [value, response, factor]
        return tuple(out)

    backwards = step_loop(steps, 4, backward, (zero, zero, one) * planes)

    inner = []
    for p in range(planes):
        local_f = forwards[2 * p]
        local_b, response, product = backwards[3 * p : 3 * p + 3]
        pi, li = product, local_f
        for d in (1, 2, 4):
            ok = row >= d
            lp = jnp.where(ok, pltpu.roll(li, d, 0), 0.0)
            pp = jnp.where(ok, pltpu.roll(pi, d, 0), 1.0)
            li, pi = pi * lp + li, pi * pp
        pf = jnp.where(row >= 1, pltpu.roll(pi, 1, 0), 1.0)
        lf = jnp.where(row >= 1, pltpu.roll(li, 1, 0), 0.0)
        pb, cb, qb = product, local_b + response * lf, response * pf
        for d in (1, 2, 4):
            ok = row < SUB - d
            cp = jnp.where(ok, pltpu.roll(cb, SUB - d, 0), 0.0)
            qp = jnp.where(ok, pltpu.roll(qb, SUB - d, 0), 0.0)
            pp = jnp.where(ok, pltpu.roll(pb, SUB - d, 0), 1.0)
            cb, qb, pb = pb * cp + cb, pb * qp + qb, pb * pp
        ok = row < SUB - 1
        summaries.append((pb[0:1], li[SUB - 1 : SUB], cb[0:1], qb[0:1]))
        inner.append(
            (
                pf,
                lf,
                jnp.where(ok, pltpu.roll(pb, SUB - 1, 0), 1.0),
                jnp.where(ok, pltpu.roll(cb, SUB - 1, 0), 0.0),
                jnp.where(ok, pltpu.roll(qb, SUB - 1, 0), 0.0),
            )
        )
    own_alpha = jnp.concatenate([1.0 / keep_ref[p, 0, 0:1] for p in range(planes)], axis=0)
    own_eps = jnp.concatenate([1.0 / s_ref[p, levels - 1 : levels, :] for p in range(planes)], axis=0)
    at_bottom, at_top = level == 0, level == gy - 1
    blocks = [jnp.concatenate([summaries[p][c] for p in range(planes)], axis=0) for c in range(4)]
    blocks[0] = blocks[0] * jnp.where(at_bottom, own_alpha, jnp.where(at_top, own_eps, 1.0))
    summary = jnp.concatenate(blocks, axis=0)
    send_s[...] = summary
    recv_s[level] = summary

    @pl.loop(1, gy)
    def _(d):
        copy_s(lax.rem(level + d, gy)).start()

    @pl.when(is_role)
    def _():
        pltpu.make_async_copy(recv_a.at[pl.ds(0, nyc - 1)], recv_a.at[pl.ds(0, nyc - 1)], a_recv).wait()
        part = recv_a[0]
        for i in range(1, nyc):
            part = part + recv_a[i]
        for x in range(nx):
            send_b[x] = part[2 * x : 2 * x + 2, :]
        recv_b[role * nx + xx] = send_b[xx]
        for y in range(gy):

            def send_level(y=y):
                for d in sorted(range(1, nx), key=lambda d: -min(d, nx - d)):
                    copy_b(lax.rem(xx + d, nx), y).start()

                @pl.when(level != y)
                def _(y=y):
                    copy_b(xx, y).start()

            if y:
                send_level()
            else:
                pl.when(jnp.logical_not(is_high))(send_level)

    pltpu.make_async_copy(recv_s.at[pl.ds(0, gy - 1)], recv_s.at[pl.ds(0, gy - 1)], s_recv).wait()

    def block(g, c):
        return recv_s[g, 2 * c : 2 * c + 2, :]

    alphas, betas = [None, block(0, 0)], [None, block(0, 1)]
    for g in range(1, gy - 1):
        alphas.append(block(g, 0) * alphas[g])
        betas.append(block(g, 0) * betas[g] + block(g, 1))
    alpha, beta = jnp.where(at_bottom, own_alpha, 0.0), jnp.zeros_like(own_alpha)
    for g in range(1, gy):
        alpha = jnp.where(level == g, alphas[g], alpha)
        beta = jnp.where(level == g, betas[g], beta)
    top = gy - 1
    gam, dlt, eps = block(top, 3) * alphas[top], block(top, 2) + block(top, 3) * betas[top], block(top, 0)
    gamma, delta = jnp.zeros_like(own_alpha), jnp.zeros_like(own_alpha)
    epsilon = jnp.where(at_top, own_eps, 0.0)
    for g in range(gy - 2, -1, -1):
        gamma = jnp.where(level == g, gam, gamma)
        delta = jnp.where(level == g, dlt, delta)
        epsilon = jnp.where(level == g, eps, epsilon)
        if g:
            gam = block(g, 0) * gam + block(g, 3) * alphas[g]
            dlt = block(g, 0) * dlt + block(g, 2) + block(g, 3) * betas[g]
            eps = block(g, 0) * eps

    def arrive(slots):
        pltpu.make_async_copy(recv_b.at[pl.ds(0, slots)], recv_b.at[pl.ds(0, slots)], b_recv).wait()

    def gather(r):
        total = recv_b[r * nx]
        for x in range(1, nx):
            total = total + recv_b[r * nx + x]
        return total

    @pl.when(is_low)
    def _():
        arrive(3 * nx - 1)
        pltpu.make_async_copy(recv_d, recv_d, d_recv).wait()
        parts = [recv_d[i] for i in range(4)]
        for i in range(4, gz):
            parts[i % 4] = parts[i % 4] + recv_d[i]
        high_ref[...] = (parts[0] + parts[1]) + (parts[2] + parts[3])

    @pl.when(is_role & jnp.logical_not(is_low))
    def _():
        arrive(4 * nx - 1)
        high_ref[...] = gather(3)

    @pl.when(jnp.logical_not(is_role))
    def _():
        arrive(4 * nx)
        high_ref[...] = gather(3)

    stress_low = gather(0) / jnp.maximum(gather(2), 1.0)
    stress_top = high_ref[...] / jnp.maximum(gather(1), 1.0)
    f_in = alpha * stress_low + beta
    b_in = gamma * stress_low + delta + epsilon * stress_top
    for p in range(planes):
        pf, lf, pb, cb, qb = inner[p]
        below = pf * f_in[p : p + 1] + lf
        above = pb * b_in[p : p + 1] + cb + qb * f_in[p : p + 1]

        def finish(b, _, p=p, below=below, above=above):
            out_ref[p, pl.ds(b, SUB, stride=steps), :] = bl_ref[p, b] + q_ref[p, b] * below + fb_ref[p, b] * above
            return _

        step_loop(steps, steps, finish, 0)

    for copy in halo_copies:
        copy.wait_send()
    pltpu.make_async_copy(recv_s.at[pl.ds(0, gy - 1)], recv_s.at[pl.ds(0, gy - 1)], s_send).wait()

    @pl.when(is_role)
    def _():
        left_a, left_b = send_a.at[pl.ds(0, nyc - 1)], send_b.at[pl.ds(0, nx - 1)]
        pltpu.make_async_copy(left_a, left_a, a_send).wait()
        pltpu.make_async_copy(left_b, left_b, b_send).wait()
        for _ in range(gy - 2):
            pltpu.make_async_copy(send_b, send_b, b_send).wait()

    @pl.when(is_role & jnp.logical_not(is_high))
    def _():
        pltpu.make_async_copy(send_b, send_b, b_send).wait()

    @pl.when(is_high)
    def _():
        pltpu.make_async_copy(send_d, send_d, d_send).wait()


def local(gz, gy, nx, *args):
    u, v, w, s, w_in, b_in, w_mid, b_mid, w_out, cell, height, face, owner = args
    planes, levels, span = u.shape
    steps = levels // SUB
    nyc = gz // nx
    rows = cell.shape[1]
    vmem = pltpu.VMEM
    scratch = [
        vmem(u.shape, F32),
        vmem(u.shape, F32),
        vmem((2, planes, WIN, span), F32),
        vmem((3, span), F32),
        vmem((3, 1, span), F32),
        vmem((span, span), F32),
        vmem((2, rows), jnp.int32),
        vmem((2, rows), jnp.int32),
        vmem((2, rows), jnp.int32),
        vmem((1, 2 * rows), jnp.int32),
        vmem((6, span, span), F32),
        vmem((2 * span, 2 * span), BF16),
        vmem((3, planes * HMAX, span), F32),
        vmem((planes * HMAX, span), F32),
        vmem((2 * gz, 2 * span), F32),
        vmem((planes, steps, SUB, span), F32),
        vmem((planes, steps, SUB, span), F32),
        vmem((planes, steps, SUB, span), F32),
        vmem((planes, steps, SUB, span), F32),
        vmem((planes, steps, SUB, span), F32),
        vmem((planes, steps, SUB, span), F32),
        vmem((planes, steps, SUB, span), F32),
        vmem((planes, steps, SUB, span), F32),
        vmem((SUB, span), F32),
        vmem((2, SUB, span), F32),
        vmem((nyc, 2 * nx, span), F32),
        vmem((nyc, 2 * nx, span), F32),
        vmem((nx, 2, span), F32),
        vmem((4 * nx, 2, span), F32),
        vmem((gz, 2, span), F32),
        vmem((gz, 2, span), F32),
        vmem((2, span), F32),
        vmem((8, span), F32),
        vmem((gy, 8, span), F32),
        pltpu.SemaphoreType.DMA((13,)),
        pltpu.SemaphoreType.DMA((2,)),
        pltpu.SemaphoreType.DMA((2,)),
    ] + [pltpu.SemaphoreType.DMA] * 8
    operands = [
        u,
        v,
        w,
        s,
        w_in,
        b_in[None, :],
        w_mid,
        b_mid[None, :],
        w_out[None, :],
        cell,
        height,
        face,
        owner.reshape(1, 2 * rows),
    ]
    return pl.pallas_call(
        functools.partial(kernel, gz, gy, nx),
        out_shape=jax.ShapeDtypeStruct(u.shape, F32),
        in_specs=[pl.BlockSpec(memory_space=pl.ANY)] * 13,
        out_specs=pl.BlockSpec(memory_space=pltpu.VMEM),
        scratch_shapes=scratch,
        compiler_params=pltpu.CompilerParams(
            collective_id=0, has_side_effects=True, vmem_limit_bytes=40 * 2**20
        ),
    )(*[pltpu.with_memory_space_constraint(x, pltpu.HBM) for x in operands])


def solution(mesh):
    field = P(None, "gy", "gz")
    gz, gy = mesh.shape["gz"], mesh.shape["gy"]
    return jax.shard_map(
        functools.partial(local, gz, gy, 4),
        mesh=mesh,
        in_specs=(field,) * 4 + (P(),) * 5 + (P(None, "gz"),) * 3 + (P(None, "gz", None),),
        out_specs=field,
        check_vma=False,
    )
```

```python
import functools

import jax
import jax.numpy as jnp
from jax import lax
from jax.experimental import pallas as pl
from jax.experimental.pallas import tpu as pltpu
from jax.sharding import PartitionSpec as P

MESH = pl.DeviceIdType.MESH
LANES = 128
SUB = 8
WIN = 16
HMAX = 8
KB = 4096
NK = 16
F32 = jnp.float32
BF16 = jnp.bfloat16


def load_rows(ref, p, b, steps):
    return ref[p, pl.ds(b, SUB, stride=steps), :]


def step_loop(count, unroll, body, init):
    def outer(i, carry):
        for j in range(unroll):
            carry = body(i * unroll + j, carry)
        return carry

    return lax.fori_loop(0, count // unroll, outer, init)


def network(is_top, u_ref, win_ref, w_in_ref, vec_ref, w_mid_ref, cols_ref, wl_ref, samp_ref, table_ref):
    planes, levels, _ = u_ref.shape
    vectors = jnp.concatenate(
        [w_in_ref[...], vec_ref[0], vec_ref[1], vec_ref[2], jnp.zeros((2, LANES), F32)], axis=0
    )
    columns = vectors.T
    for c in range(6):
        cols_ref[c] = jnp.broadcast_to(columns[:, c : c + 1], (LANES, LANES))
    mid = w_mid_ref[...].T
    mid_hi = mid.astype(BF16)
    mid_lo = (mid - mid_hi.astype(F32)).astype(BF16)
    wl_ref[...] = jnp.concatenate(
        [jnp.concatenate([mid_hi, mid_hi], axis=1), jnp.concatenate([mid_lo, mid_lo], axis=1)], axis=0
    )
    for p in range(planes):
        samp_ref[0, p * HMAX : (p + 1) * HMAX, :] = jnp.where(
            is_top, u_ref[p, levels - 1 - HMAX : levels - 1, :], u_ref[p, 1 : 1 + HMAX, :]
        )
        for c in range(2):
            samp_ref[1 + c, p * HMAX : (p + 1) * HMAX, :] = jnp.where(
                is_top, win_ref[c, p, WIN - 1 - HMAX : WIN - 1, :], win_ref[c, p, 1 : 1 + HMAX, :]
            )

    @pl.loop(0, planes * HMAX // NK)
    def _(i):
        halves = []
        for h in range(NK):
            k = i * NK + h
            pre = cols_ref[3]
            for c in range(3):
                pre = pre + cols_ref[c] * samp_ref[c, pl.ds(k, 1), :]
            hidden = jnp.tanh(pre)
            upper = hidden.astype(BF16)
            lower = (hidden - upper.astype(F32)).astype(BF16)
            halves.append(jnp.concatenate([upper, lower], axis=0))
        mixed = jnp.dot(wl_ref[...], jnp.concatenate(halves, axis=1), preferred_element_type=F32)
        for h in range(NK):
            part = mixed[:, h * LANES : (h + 1) * LANES]
            second = jnp.tanh(part[:LANES] + part[LANES:] + cols_ref[4])
            table_ref[pl.ds(i * NK + h, 1), :] = jnp.sum(second * cols_ref[5], axis=0, keepdims=True)


def binning(is_top, nx, nyc, cell_ref, height_ref, face_ref, owner_ref, table_ref, acc_ref):
    rows = cell_ref.shape[1]
    planes = table_ref.shape[0] // HMAX
    acc_ref[...] = jnp.zeros_like(acc_ref)
    bins = acc_ref.shape[0] // 2
    row = lax.broadcasted_iota(jnp.int32, (SUB, LANES), 0)
    rows_iota = lax.broadcasted_iota(jnp.int32, (LANES, KB), 0).astype(F32).astype(BF16)
    bins_iota = lax.broadcasted_iota(jnp.int32, (bins, KB), 0).astype(F32).astype(BF16)

    @pl.loop(0, rows // KB)
    def _(i):
        at = pl.ds(pl.multiple_of(i * KB, KB), KB)

        def wall(ref):
            return jnp.where(is_top, ref[1:2, at], ref[0:1, at])

        cell, height, face = wall(cell_ref), wall(height_ref), wall(face_ref)
        owner = owner_ref[:, pl.ds(pl.multiple_of(jnp.where(is_top, rows, 0) + i * KB, KB), KB)]
        span = cell % LANES
        key = (cell // LANES) * HMAX + jnp.where(is_top, HMAX - height, height - 1)
        picks = []
        for j in range(KB // LANES):
            cut = slice(j * LANES, (j + 1) * LANES)
            index = jnp.broadcast_to(span[:, cut], (SUB, LANES))
            keyed = jnp.broadcast_to(key[:, cut], (SUB, LANES))
            value = jnp.zeros((SUB, LANES), F32)
            for t in range(planes):
                got = jnp.take_along_axis(table_ref[t * HMAX : (t + 1) * HMAX, :], index, axis=1)
                value = value + jnp.where(keyed == row + t * HMAX, got, 0.0)
            picks.append(jnp.sum(value, axis=0, keepdims=True))
        value = jnp.concatenate(picks, axis=1)
        first = value.astype(BF16).astype(F32)
        rest = value - first
        low = face % LANES
        high = (owner % nyc) * (2 * nx) + (owner // nyc) * 2 + face // LANES
        named = bins_iota == high.astype(F32).astype(BF16)
        carried = jnp.concatenate(
            [jnp.where(named, first.astype(BF16), BF16(0.0)), jnp.where(named, rest.astype(BF16), BF16(0.0))], axis=0
        )
        onto = jnp.where(rows_iota == low.astype(F32).astype(BF16), BF16(1.0), BF16(0.0))
        acc_ref[...] += lax.dot_general(
            carried, onto, (((1,), (1,)), ((), ())), preferred_element_type=F32
        )


def kernel(
    gz,
    gy,
    nx,
    u_hbm,
    v_hbm,
    w_hbm,
    s_hbm,
    w_in_hbm,
    b_in_hbm,
    w_mid_hbm,
    b_mid_hbm,
    w_out_hbm,
    cell_hbm,
    height_hbm,
    face_hbm,
    owner_hbm,
    out_ref,
    u_ref,
    s_ref,
    win_ref,
    w_in_ref,
    vec_ref,
    w_mid_ref,
    cell_ref,
    height_ref,
    face_ref,
    owner_ref,
    cols_ref,
    wl_ref,
    samp_ref,
    table_ref,
    acc_ref,
    keep_ref,
    gain_ref,
    gsrc_ref,
    lf_ref,
    ff_ref,
    bl_ref,
    q_ref,
    fb_ref,
    pack_ref,
    halo_ref,
    send_a,
    recv_a,
    send_b,
    recv_b,
    send_d,
    recv_d,
    high_ref,
    send_s,
    recv_s,
    load_sem,
    halo_send,
    halo_recv,
    a_send,
    a_recv,
    b_send,
    b_recv,
    d_send,
    d_recv,
    s_send,
    s_recv,
    ready,
):
    planes, levels, _ = u_ref.shape
    steps = levels // SUB
    total_steps = planes * steps
    nyc = gz // nx
    me = lax.axis_index("gz")
    level = lax.axis_index("gy")
    xx = me // nyc
    yc = me % nyc
    is_low, is_high = level == 0, level == gy - 1
    is_top = (level == 1) | is_high
    is_tot = is_low | is_high
    is_early, is_direct = level <= 2, level <= 1
    is_role = is_early | is_high
    role = jnp.where(is_high, 3, level)
    roles = (0, 1, 2, gy - 1)

    start = pl.multiple_of(jnp.where(is_top, levels - WIN, 0), 8)
    load_u = pltpu.make_async_copy(u_hbm, u_ref, load_sem.at[0])
    load_s = pltpu.make_async_copy(s_hbm, s_ref, load_sem.at[1])
    lists = [
        pltpu.make_async_copy(src, dst, load_sem.at[2 + i])
        for i, (src, dst) in enumerate(
            [(cell_hbm, cell_ref), (height_hbm, height_ref), (face_hbm, face_ref), (owner_hbm, owner_ref)]
        )
    ]
    weights = [
        pltpu.make_async_copy(src, dst, load_sem.at[6 + i])
        for i, (src, dst) in enumerate(
            [
                (w_in_hbm, w_in_ref),
                (b_in_hbm, vec_ref.at[0]),
                (b_mid_hbm, vec_ref.at[1]),
                (w_out_hbm, vec_ref.at[2]),
                (w_mid_hbm, w_mid_ref),
                (v_hbm.at[:, pl.ds(start, WIN), :], win_ref.at[0]),
                (w_hbm.at[:, pl.ds(start, WIN), :], win_ref.at[1]),
            ]
        )
    ]
    load_u.start()

    @pl.when(is_tot)
    def _():
        for copy in weights:
            copy.start()

    @pl.when(is_role)
    def _():
        for copy in lists:
            copy.start()

    load_s.start()

    barrier = pltpu.get_barrier_semaphore()

    def greet(z, y):
        pl.semaphore_signal(barrier, inc=1, device_id=(z, y), device_id_type=MESH)

    left, right = lax.rem(me + gz - 1, gz), lax.rem(me + 1, gz)
    greet(left, level)
    greet(right, level)

    @pl.when(is_early)
    def _():
        @pl.loop(1, nx)
        def _(d):
            for y in range(3):
                greet(lax.rem(xx + d, nx) * nyc + yc, y)

    @pl.when(is_role)
    def _():
        @pl.loop(1, nyc)
        def _(d):
            greet(xx * nyc + lax.rem(yc + d, nyc), level)

    for y in range(gy):
        meets = (level != y) if y >= 3 else is_early & (level != y)

        @pl.when(meets)
        def _(y=y):
            greet(me, y)

    @pl.when(is_early)
    def _():
        @pl.loop(1, nx)
        def _(d):
            for y in range(3, gy - 1):
                greet(lax.rem(xx + d, nx) * nyc + yc, y)

    @pl.when(jnp.logical_not(is_direct))
    def _():
        @pl.loop(1, nx)
        def _(d):
            greet(lax.rem(xx + d, nx) * nyc + yc, gy - 1)

    @pl.when(is_direct)
    def _():
        @pl.loop(1, gz)
        def _(d):
            greet(lax.rem(me + d, gz), gy - 1)

    lane = lax.broadcasted_iota(jnp.int32, (SUB, LANES), 1)
    row = lax.broadcasted_iota(jnp.int32, (SUB, LANES), 0)
    load_u.wait()
    packed = jnp.zeros((SUB, LANES), F32)
    for p in range(planes):

        def pack(b, acc, p=p):
            i = p * steps + b
            return jnp.where(lane // 2 == i, pltpu.roll(load_rows(u_ref, p, b, steps), 2 * i + 1, 1), acc)

        packed = step_loop(steps, 8, pack, packed)
    pack_ref[...] = packed

    @pl.when(is_tot)
    def _():
        for copy in weights:
            copy.wait()
        network(is_top, u_ref, win_ref, w_in_ref, vec_ref, w_mid_ref, cols_ref, wl_ref, samp_ref, table_ref)

    @pl.when(is_role & jnp.logical_not(is_tot))
    def _():
        table_ref[...] = jnp.ones_like(table_ref)

    @pl.when(is_role)
    def _():
        for copy in lists:
            copy.wait()
        binning(is_top, nx, nyc, cell_ref, height_ref, face_ref, owner_ref, table_ref, acc_ref)

    base = gy - 1 + 2

    @pl.when(is_early)
    def _():
        pl.semaphore_wait(barrier, 4 + nyc - 1 + (nx - 1) * 3)

    @pl.when(is_high)
    def _():
        pl.semaphore_wait(barrier, base + nyc - 1 + (nx - 1) * (gy - 2) + 2 * (gz - 1))

    @pl.when(jnp.logical_not(is_role))
    def _():
        pl.semaphore_wait(barrier, base + (nx - 1) * 3)

    @pl.when(jnp.logical_not(is_early))
    def _():
        for y in range(3):
            for d in range(nx):
                pl.semaphore_signal(
                    ready, inc=1, device_id=(lax.rem(xx + d, nx) * nyc + yc, y), device_id_type=MESH
                )

    halo_copies = [
        pltpu.make_async_remote_copy(
            src_ref=pack_ref,
            dst_ref=halo_ref.at[slot],
            send_sem=halo_send.at[slot],
            recv_sem=halo_recv.at[slot],
            device_id=(z, level),
            device_id_type=MESH,
        )
        for slot, z in ((0, right), (1, left))
    ]
    for copy in halo_copies:
        copy.start()

    def copy_a(z, slot):
        return pltpu.make_async_remote_copy(
            src_ref=send_a.at[z],
            dst_ref=recv_a.at[slot],
            send_sem=a_send,
            recv_sem=a_recv,
            device_id=(xx * nyc + z, level),
            device_id_type=MESH,
        )

    def copy_b(x, y):
        return pltpu.make_async_remote_copy(
            src_ref=send_b.at[x],
            dst_ref=recv_b.at[role * nx + xx],
            send_sem=b_send,
            recv_sem=b_recv,
            device_id=(x * nyc + yc, y),
            device_id_type=MESH,
        )

    def copy_d(x, z, y):
        return pltpu.make_async_remote_copy(
            src_ref=send_d.at[z * nx + x],
            dst_ref=recv_d.at[me],
            send_sem=d_send,
            recv_sem=d_recv,
            device_id=(x * nyc + z, y),
            device_id_type=MESH,
        )

    def copy_s(y):
        return pltpu.make_async_remote_copy(
            src_ref=send_s,
            dst_ref=recv_s.at[level],
            send_sem=s_send,
            recv_sem=s_recv,
            device_id=(me, y),
            device_id_type=MESH,
        )

    @pl.when(is_role)
    def _():
        binned = acc_ref[: 2 * gz, :] + acc_ref[2 * gz :, :]

        send_a[...] = binned.reshape(send_a.shape)
        recv_a[yc] = send_a[yc]

    ny = nyc // 2
    early = list(range(-(-ny // 2))) + list(range(ny - 1, -(-ny // 2) - 1, -1))

    @pl.when(is_high)
    def _():
        send_d[...] = (acc_ref[: 2 * gz, :] + acc_ref[2 * gz :, :]).reshape(send_d.shape)
        for x in range(nx):
            for c in (1, 0):
                copy_d(x, 2 * early[0] + c, 0).start()

    @pl.when(is_role)
    def _():
        for d in sorted(range(1, nyc), key=lambda d: -min(d, nyc - d)):
            copy_a(lax.rem(yc + d, nyc), yc).start()

    @pl.when(is_high)
    def _():
        for x in range(nx):
            for c in (1, 0):
                copy_d(x, 2 * early[0] + c, 1).start()
        for y in early[1:]:
            for level_to in range(2):
                for x in range(nx):
                    for c in (1, 0):
                        copy_d(x, 2 * y + c, level_to).start()

    load_s.wait()
    for copy in halo_copies:
        copy.wait_recv()
    merged = jnp.where(lane % 2 == 1, pltpu.roll(halo_ref[0], 1, 1), pltpu.roll(halo_ref[1], LANES - 1, 1))
    zero, one = jnp.zeros((SUB, LANES), F32), jnp.ones((SUB, LANES), F32)
    summaries = []
    for p in range(planes):

        def prepare(b, _, p=p):
            i = p * steps + b
            stiff = load_rows(s_ref, p, b, steps)
            here = load_rows(u_ref, p, b, steps)
            halo = pltpu.roll(merged, LANES - 1 - 2 * i, 1)
            before = jnp.where(lane == 0, halo, pltpu.roll(here, 1, 1))
            after = jnp.where(lane == LANES - 1, halo, pltpu.roll(here, LANES - 1, 1))
            source = here + 0.2 * (after + before - 2.0 * here)
            gain = 1.0 / (1.0 + stiff)
            keep_ref[p, b] = stiff * gain
            gain_ref[p, b] = gain
            gsrc_ref[p, b] = gain * source
            return _

        step_loop(steps, 4, prepare, 0)

    def forward(b, carry):
        out = []
        for p in range(planes):
            value, factor = carry[2 * p : 2 * p + 2]
            keep = keep_ref[p, b]
            value = keep * value + gsrc_ref[p, b]
            factor = keep * factor
            lf_ref[p, b] = value
            ff_ref[p, b] = factor
            out += [value, factor]
        return tuple(out)

    forwards = step_loop(steps, 4, forward, (zero, one) * planes)

    def backward(t, carry):
        out = []
        b = steps - 1 - t
        for p in range(planes):
            value, response, factor = carry[3 * p : 3 * p + 3]
            keep, gain = keep_ref[p, b], gain_ref[p, b]
            value = keep * value + gain * lf_ref[p, b]
            response = keep * response + gain * ff_ref[p, b]
            factor = keep * factor
            at = pl.ds(b, SUB, stride=steps)
            bl_ref[p, at, :] = value
            q_ref[p, at, :] = response
            fb_ref[p, at, :] = factor
            out += [value, response, factor]
        return tuple(out)

    backwards = step_loop(steps, 4, backward, (zero, zero, one) * planes)

    inner = []
    for p in range(planes):
        local_f = forwards[2 * p]
        local_b, response, product = backwards[3 * p : 3 * p + 3]
        pi, li = product, local_f
        for d in (1, 2, 4):
            ok = row >= d
            lp = jnp.where(ok, pltpu.roll(li, d, 0), 0.0)
            pp = jnp.where(ok, pltpu.roll(pi, d, 0), 1.0)
            li, pi = pi * lp + li, pi * pp
        pf = jnp.where(row >= 1, pltpu.roll(pi, 1, 0), 1.0)
        lf = jnp.where(row >= 1, pltpu.roll(li, 1, 0), 0.0)
        pb, cb, qb = product, local_b + response * lf, response * pf
        for d in (1, 2, 4):
            ok = row < SUB - d
            cp = jnp.where(ok, pltpu.roll(cb, SUB - d, 0), 0.0)
            qp = jnp.where(ok, pltpu.roll(qb, SUB - d, 0), 0.0)
            pp = jnp.where(ok, pltpu.roll(pb, SUB - d, 0), 1.0)
            cb, qb, pb = pb * cp + cb, pb * qp + qb, pb * pp
        ok = row < SUB - 1
        summaries.append((pb[0:1], li[SUB - 1 : SUB], cb[0:1], qb[0:1]))
        inner.append(
            (
                pf,
                lf,
                jnp.where(ok, pltpu.roll(pb, SUB - 1, 0), 1.0),
                jnp.where(ok, pltpu.roll(cb, SUB - 1, 0), 0.0),
                jnp.where(ok, pltpu.roll(qb, SUB - 1, 0), 0.0),
            )
        )
    own_alpha = jnp.concatenate([1.0 / keep_ref[p, 0, 0:1] for p in range(planes)], axis=0)
    own_eps = jnp.concatenate([1.0 / s_ref[p, levels - 1 : levels, :] for p in range(planes)], axis=0)
    at_bottom, at_top = level == 0, level == gy - 1
    blocks = [jnp.concatenate([summaries[p][c] for p in range(planes)], axis=0) for c in range(4)]
    blocks[0] = blocks[0] * jnp.where(at_bottom, own_alpha, jnp.where(at_top, own_eps, 1.0))
    summary = jnp.concatenate(blocks, axis=0)
    send_s[...] = summary
    recv_s[level] = summary

    def summary_to(levels_to):
        for y in levels_to:

            @pl.when(level != y)
            def _(y=y):
                copy_s(y).start()

    def second_to(levels_to):
        for y in levels_to:
            for d in sorted(range(1, nx), key=lambda d: -min(d, nx - d)):
                copy_b(lax.rem(xx + d, nx), y).start()

            @pl.when(level != y)
            def _(y=y):
                copy_b(xx, y).start()

    summary_to(range(3))

    @pl.when(jnp.logical_not(is_early))
    def _():
        summary_to(range(3, gy))

    @pl.when(is_role)
    def _():
        pltpu.make_async_copy(recv_a.at[pl.ds(0, nyc - 1)], recv_a.at[pl.ds(0, nyc - 1)], a_recv).wait()
        part = recv_a[0]
        for i in range(1, nyc):
            part = part + recv_a[i]
        for x in range(nx):
            send_b[x] = part[2 * x : 2 * x + 2, :]
        recv_b[role * nx + xx] = send_b[xx]

    @pl.when(is_early)
    def _():
        second_to(range(3))
        pl.semaphore_wait(ready, nx * (gy - 3))
        summary_to(range(3, gy))
        second_to(range(3, gy))

    @pl.when(is_high)
    def _():
        second_to(range(2, gy))

    pltpu.make_async_copy(recv_s.at[pl.ds(0, gy - 1)], recv_s.at[pl.ds(0, gy - 1)], s_recv).wait()

    def block(g, c):
        return recv_s[g, 2 * c : 2 * c + 2, :]

    alphas, betas = [None, block(0, 0)], [None, block(0, 1)]
    for g in range(1, gy - 1):
        alphas.append(block(g, 0) * alphas[g])
        betas.append(block(g, 0) * betas[g] + block(g, 1))
    alpha, beta = jnp.where(at_bottom, own_alpha, 0.0), jnp.zeros_like(own_alpha)
    for g in range(1, gy):
        alpha = jnp.where(level == g, alphas[g], alpha)
        beta = jnp.where(level == g, betas[g], beta)
    top = gy - 1
    gam, dlt, eps = block(top, 3) * alphas[top], block(top, 2) + block(top, 3) * betas[top], block(top, 0)
    gamma, delta = jnp.zeros_like(own_alpha), jnp.zeros_like(own_alpha)
    epsilon = jnp.where(at_top, own_eps, 0.0)
    for g in range(gy - 2, -1, -1):
        gamma = jnp.where(level == g, gam, gamma)
        delta = jnp.where(level == g, dlt, delta)
        epsilon = jnp.where(level == g, eps, epsilon)
        if g:
            gam = block(g, 0) * gam + block(g, 3) * alphas[g]
            dlt = block(g, 0) * dlt + block(g, 2) + block(g, 3) * betas[g]
            eps = block(g, 0) * eps

    def arrive(slots):
        pltpu.make_async_copy(recv_b.at[pl.ds(0, slots)], recv_b.at[pl.ds(0, slots)], b_recv).wait()

    def gather(r):
        total = recv_b[r * nx]
        for x in range(1, nx):
            total = total + recv_b[r * nx + x]
        return total

    @pl.when(is_direct)
    def _():
        arrive(3 * nx - 1)
        pltpu.make_async_copy(recv_d, recv_d, d_recv).wait()
        parts = [recv_d[i] for i in range(4)]
        for i in range(4, gz):
            parts[i % 4] = parts[i % 4] + recv_d[i]
        high_ref[...] = (parts[0] + parts[1]) + (parts[2] + parts[3])

    @pl.when(is_role & jnp.logical_not(is_direct))
    def _():
        arrive(4 * nx - 1)
        high_ref[...] = gather(3)

    @pl.when(jnp.logical_not(is_role))
    def _():
        arrive(4 * nx)
        high_ref[...] = gather(3)

    stress_low = gather(0) / jnp.maximum(gather(2), 1.0)
    stress_top = high_ref[...] / jnp.maximum(gather(1), 1.0)
    f_in = alpha * stress_low + beta
    b_in = gamma * stress_low + delta + epsilon * stress_top
    for p in range(planes):
        pf, lf, pb, cb, qb = inner[p]
        below = pf * f_in[p : p + 1] + lf
        above = pb * b_in[p : p + 1] + cb + qb * f_in[p : p + 1]

        for j in range(SUB):
            cut = slice(j * steps, (j + 1) * steps)
            out_ref[p, cut, :] = (
                bl_ref[p, cut, :] + q_ref[p, cut, :] * below[j : j + 1] + fb_ref[p, cut, :] * above[j : j + 1]
            )

    for copy in halo_copies:
        copy.wait_send()
    pltpu.make_async_copy(recv_s.at[pl.ds(0, gy - 1)], recv_s.at[pl.ds(0, gy - 1)], s_send).wait()

    @pl.when(is_role)
    def _():
        left_a, left_b = send_a.at[pl.ds(0, nyc - 1)], send_b.at[pl.ds(0, nx - 1)]
        pltpu.make_async_copy(left_a, left_a, a_send).wait()
        pltpu.make_async_copy(left_b, left_b, b_send).wait()
        for _ in range(gy - 3):
            pltpu.make_async_copy(send_b, send_b, b_send).wait()

    @pl.when(is_early)
    def _():
        for _ in range(2):
            pltpu.make_async_copy(send_b, send_b, b_send).wait()

    @pl.when(is_high)
    def _():
        for _ in range(2):
            pltpu.make_async_copy(send_d, send_d, d_send).wait()


def local(gz, gy, nx, *args):
    u, v, w, s, w_in, b_in, w_mid, b_mid, w_out, cell, height, face, owner = args
    planes, levels, span = u.shape
    steps = levels // SUB
    nyc = gz // nx
    rows = cell.shape[1]
    vmem = pltpu.VMEM
    scratch = [
        vmem(u.shape, F32),
        vmem(u.shape, F32),
        vmem((2, planes, WIN, span), F32),
        vmem((3, span), F32),
        vmem((3, 1, span), F32),
        vmem((span, span), F32),
        vmem((2, rows), jnp.int32),
        vmem((2, rows), jnp.int32),
        vmem((2, rows), jnp.int32),
        vmem((1, 2 * rows), jnp.int32),
        vmem((6, span, span), F32),
        vmem((2 * span, 2 * span), BF16),
        vmem((3, planes * HMAX, span), F32),
        vmem((planes * HMAX, span), F32),
        vmem((4 * gz, span), F32),
        vmem((planes, steps, SUB, span), F32),
        vmem((planes, steps, SUB, span), F32),
        vmem((planes, steps, SUB, span), F32),
        vmem((planes, steps, SUB, span), F32),
        vmem((planes, steps, SUB, span), F32),
        vmem(u.shape, F32),
        vmem(u.shape, F32),
        vmem(u.shape, F32),
        vmem((SUB, span), F32),
        vmem((2, SUB, span), F32),
        vmem((nyc, 2 * nx, span), F32),
        vmem((nyc, 2 * nx, span), F32),
        vmem((nx, 2, span), F32),
        vmem((4 * nx, 2, span), F32),
        vmem((gz, 2, span), F32),
        vmem((gz, 2, span), F32),
        vmem((2, span), F32),
        vmem((8, span), F32),
        vmem((gy, 8, span), F32),
        pltpu.SemaphoreType.DMA((13,)),
        pltpu.SemaphoreType.DMA((2,)),
        pltpu.SemaphoreType.DMA((2,)),
    ] + [pltpu.SemaphoreType.DMA] * 8 + [pltpu.SemaphoreType.REGULAR]
    operands = [
        u,
        v,
        w,
        s,
        w_in,
        b_in[None, :],
        w_mid,
        b_mid[None, :],
        w_out[None, :],
        cell,
        height,
        face,
        owner.reshape(1, 2 * rows),
    ]
    return pl.pallas_call(
        functools.partial(kernel, gz, gy, nx),
        out_shape=jax.ShapeDtypeStruct(u.shape, F32),
        in_specs=[pl.BlockSpec(memory_space=pl.ANY)] * 13,
        out_specs=pl.BlockSpec(memory_space=pltpu.VMEM),
        scratch_shapes=scratch,
        compiler_params=pltpu.CompilerParams(
            collective_id=0, has_side_effects=True, vmem_limit_bytes=40 * 2**20
        ),
    )(*[pltpu.with_memory_space_constraint(x, pltpu.HBM) for x in operands])


def solution(mesh):
    field = P(None, "gy", "gz")
    gz, gy = mesh.shape["gz"], mesh.shape["gy"]
    return jax.shard_map(
        functools.partial(local, gz, gy, 4),
        mesh=mesh,
        in_specs=(field,) * 4 + (P(),) * 5 + (P(None, "gz"),) * 3 + (P(None, "gz", None),),
        out_specs=field,
        check_vma=False,
    )
```

```python
import functools

import jax
import jax.numpy as jnp
from jax import lax
from jax.experimental import pallas as pl
from jax.experimental.pallas import tpu as pltpu
from jax.sharding import PartitionSpec as P

MESH = pl.DeviceIdType.MESH
LANES = 128
SUB = 8
WIN = 16
HMAX = 8
KB = 4096
NK = 16
F32 = jnp.float32
BF16 = jnp.bfloat16


def load_rows(ref, p, b, steps):
    return ref[p, pl.ds(b, SUB, stride=steps), :]


def step_loop(count, unroll, body, init):
    def outer(i, carry):
        for j in range(unroll):
            carry = body(i * unroll + j, carry)
        return carry

    return lax.fori_loop(0, count // unroll, outer, init)


def network(is_top, u_ref, win_ref, w_in_ref, vec_ref, w_mid_ref, cols_ref, wl_ref, samp_ref, table_ref):
    planes, levels, _ = u_ref.shape
    vectors = jnp.concatenate(
        [w_in_ref[...], vec_ref[0], vec_ref[1], vec_ref[2], jnp.zeros((2, LANES), F32)], axis=0
    )
    columns = vectors.T
    for c in range(6):
        cols_ref[c] = jnp.broadcast_to(columns[:, c : c + 1], (LANES, LANES))
    mid = w_mid_ref[...].T
    mid_hi = mid.astype(BF16)
    mid_lo = (mid - mid_hi.astype(F32)).astype(BF16)
    wl_ref[...] = jnp.concatenate(
        [jnp.concatenate([mid_hi, mid_hi], axis=1), jnp.concatenate([mid_lo, mid_lo], axis=1)], axis=0
    )
    for p in range(planes):
        samp_ref[0, p * HMAX : (p + 1) * HMAX, :] = jnp.where(
            is_top, u_ref[p, levels - 1 - HMAX : levels - 1, :], u_ref[p, 1 : 1 + HMAX, :]
        )
        for c in range(2):
            samp_ref[1 + c, p * HMAX : (p + 1) * HMAX, :] = jnp.where(
                is_top, win_ref[c, p, WIN - 1 - HMAX : WIN - 1, :], win_ref[c, p, 1 : 1 + HMAX, :]
            )

    @pl.loop(0, planes * HMAX // NK)
    def _(i):
        halves = []
        for h in range(NK):
            k = i * NK + h
            pre = cols_ref[3]
            for c in range(3):
                pre = pre + cols_ref[c] * samp_ref[c, pl.ds(k, 1), :]
            hidden = jnp.tanh(pre)
            upper = hidden.astype(BF16)
            lower = (hidden - upper.astype(F32)).astype(BF16)
            halves.append(jnp.concatenate([upper, lower], axis=0))
        mixed = jnp.dot(wl_ref[...], jnp.concatenate(halves, axis=1), preferred_element_type=F32)
        for h in range(NK):
            part = mixed[:, h * LANES : (h + 1) * LANES]
            second = jnp.tanh(part[:LANES] + part[LANES:] + cols_ref[4])
            table_ref[pl.ds(i * NK + h, 1), :] = jnp.sum(second * cols_ref[5], axis=0, keepdims=True)


def binning(is_top, nx, nyc, cell_ref, height_ref, face_ref, owner_ref, table_ref, acc_ref):
    rows = cell_ref.shape[1]
    planes = table_ref.shape[0] // HMAX
    acc_ref[...] = jnp.zeros_like(acc_ref)
    bins = acc_ref.shape[0] // 2
    row = lax.broadcasted_iota(jnp.int32, (SUB, LANES), 0)
    rows_iota = lax.broadcasted_iota(jnp.int32, (LANES, KB), 0).astype(F32).astype(BF16)
    bins_iota = lax.broadcasted_iota(jnp.int32, (bins, KB), 0).astype(F32).astype(BF16)

    @pl.loop(0, rows // KB)
    def _(i):
        at = pl.ds(pl.multiple_of(i * KB, KB), KB)

        def wall(ref):
            return jnp.where(is_top, ref[1:2, at], ref[0:1, at])

        cell, height, face = wall(cell_ref), wall(height_ref), wall(face_ref)
        owner = owner_ref[:, pl.ds(pl.multiple_of(jnp.where(is_top, rows, 0) + i * KB, KB), KB)]
        span = cell % LANES
        key = (cell // LANES) * HMAX + jnp.where(is_top, HMAX - height, height - 1)
        picks = []
        for j in range(KB // LANES):
            cut = slice(j * LANES, (j + 1) * LANES)
            index = jnp.broadcast_to(span[:, cut], (SUB, LANES))
            keyed = jnp.broadcast_to(key[:, cut], (SUB, LANES))
            value = jnp.zeros((SUB, LANES), F32)
            for t in range(planes):
                got = jnp.take_along_axis(table_ref[t * HMAX : (t + 1) * HMAX, :], index, axis=1)
                value = value + jnp.where(keyed == row + t * HMAX, got, 0.0)
            picks.append(jnp.sum(value, axis=0, keepdims=True))
        value = jnp.concatenate(picks, axis=1)
        first = value.astype(BF16).astype(F32)
        rest = value - first
        low = face % LANES
        high = (owner % nyc) * (2 * nx) + (owner // nyc) * 2 + face // LANES
        named = bins_iota == high.astype(F32).astype(BF16)
        carried = jnp.concatenate(
            [jnp.where(named, first.astype(BF16), BF16(0.0)), jnp.where(named, rest.astype(BF16), BF16(0.0))], axis=0
        )
        onto = jnp.where(rows_iota == low.astype(F32).astype(BF16), BF16(1.0), BF16(0.0))
        acc_ref[...] += lax.dot_general(
            carried, onto, (((1,), (1,)), ((), ())), preferred_element_type=F32
        )


def kernel(
    gz,
    gy,
    nx,
    u_hbm,
    v_hbm,
    w_hbm,
    s_hbm,
    w_in_hbm,
    b_in_hbm,
    w_mid_hbm,
    b_mid_hbm,
    w_out_hbm,
    cell_hbm,
    height_hbm,
    face_hbm,
    owner_hbm,
    out_ref,
    u_ref,
    s_ref,
    win_ref,
    w_in_ref,
    vec_ref,
    w_mid_ref,
    cell_ref,
    height_ref,
    face_ref,
    owner_ref,
    cols_ref,
    wl_ref,
    samp_ref,
    table_ref,
    acc_ref,
    keep_ref,
    gain_ref,
    gsrc_ref,
    lf_ref,
    ff_ref,
    bl_ref,
    q_ref,
    fb_ref,
    pack_ref,
    halo_ref,
    send_a,
    recv_a,
    send_b,
    recv_b,
    send_d,
    recv_d,
    high_ref,
    send_s,
    recv_s,
    load_sem,
    halo_send,
    halo_recv,
    a_send,
    a_recv,
    b_send,
    b_recv,
    d_send,
    d_recv,
    s_send,
    s_recv,
    ready,
):
    planes, levels, _ = u_ref.shape
    steps = levels // SUB
    total_steps = planes * steps
    nyc = gz // nx
    me = lax.axis_index("gz")
    level = lax.axis_index("gy")
    xx = me // nyc
    yc = me % nyc
    is_low, is_high = level == 0, level == gy - 1
    is_top = (level == 1) | is_high
    is_tot = is_low | is_high
    is_early, is_direct = level <= 2, level <= 1
    is_role = is_early | is_high
    role = jnp.where(is_high, 3, level)
    roles = (0, 1, 2, gy - 1)

    start = pl.multiple_of(jnp.where(is_top, levels - WIN, 0), 8)
    load_u = pltpu.make_async_copy(u_hbm, u_ref, load_sem.at[0])
    load_s = pltpu.make_async_copy(s_hbm, s_ref, load_sem.at[1])
    lists = [
        pltpu.make_async_copy(src, dst, load_sem.at[2 + i])
        for i, (src, dst) in enumerate(
            [(cell_hbm, cell_ref), (height_hbm, height_ref), (face_hbm, face_ref), (owner_hbm, owner_ref)]
        )
    ]
    weights = [
        pltpu.make_async_copy(src, dst, load_sem.at[6 + i])
        for i, (src, dst) in enumerate(
            [
                (w_in_hbm, w_in_ref),
                (b_in_hbm, vec_ref.at[0]),
                (b_mid_hbm, vec_ref.at[1]),
                (w_out_hbm, vec_ref.at[2]),
                (w_mid_hbm, w_mid_ref),
                (v_hbm.at[:, pl.ds(start, WIN), :], win_ref.at[0]),
                (w_hbm.at[:, pl.ds(start, WIN), :], win_ref.at[1]),
            ]
        )
    ]
    load_u.start()

    @pl.when(is_tot)
    def _():
        for copy in weights:
            copy.start()

    @pl.when(is_role)
    def _():
        for copy in lists:
            copy.start()

    load_s.start()

    barrier = pltpu.get_barrier_semaphore()

    def greet(z, y):
        pl.semaphore_signal(barrier, inc=1, device_id=(z, y), device_id_type=MESH)

    left, right = lax.rem(me + gz - 1, gz), lax.rem(me + 1, gz)
    greet(left, level)
    greet(right, level)

    @pl.when(is_early)
    def _():
        @pl.loop(1, nx)
        def _(d):
            for y in range(3):
                greet(lax.rem(xx + d, nx) * nyc + yc, y)

    @pl.when(is_role)
    def _():
        @pl.loop(1, nyc)
        def _(d):
            greet(xx * nyc + lax.rem(yc + d, nyc), level)

    for y in range(gy):
        meets = (level != y) if y >= 3 else is_early & (level != y)

        @pl.when(meets)
        def _(y=y):
            greet(me, y)

    @pl.when(is_early)
    def _():
        @pl.loop(1, nx)
        def _(d):
            for y in range(3, gy - 1):
                greet(lax.rem(xx + d, nx) * nyc + yc, y)

    @pl.when(jnp.logical_not(is_direct))
    def _():
        @pl.loop(1, nx)
        def _(d):
            greet(lax.rem(xx + d, nx) * nyc + yc, gy - 1)

    @pl.when(is_direct)
    def _():
        @pl.loop(1, gz)
        def _(d):
            greet(lax.rem(me + d, gz), gy - 1)

    lane = lax.broadcasted_iota(jnp.int32, (SUB, LANES), 1)
    row = lax.broadcasted_iota(jnp.int32, (SUB, LANES), 0)
    load_u.wait()
    packed = jnp.zeros((SUB, LANES), F32)
    for p in range(planes):

        def pack(b, acc, p=p):
            i = p * steps + b
            return jnp.where(lane // 2 == i, pltpu.roll(load_rows(u_ref, p, b, steps), 2 * i + 1, 1), acc)

        packed = step_loop(steps, 8, pack, packed)
    pack_ref[...] = packed

    @pl.when(is_tot)
    def _():
        for copy in weights:
            copy.wait()
        network(is_top, u_ref, win_ref, w_in_ref, vec_ref, w_mid_ref, cols_ref, wl_ref, samp_ref, table_ref)

    @pl.when(is_role & jnp.logical_not(is_tot))
    def _():
        table_ref[...] = jnp.ones_like(table_ref)

    @pl.when(is_role)
    def _():
        for copy in lists:
            copy.wait()
        binning(is_top, nx, nyc, cell_ref, height_ref, face_ref, owner_ref, table_ref, acc_ref)

    base = gy - 1 + 2

    @pl.when(is_early)
    def _():
        pl.semaphore_wait(barrier, 4 + nyc - 1 + (nx - 1) * 3)

    @pl.when(is_high)
    def _():
        pl.semaphore_wait(barrier, base + nyc - 1 + (nx - 1) * (gy - 2) + 2 * (gz - 1))

    @pl.when(jnp.logical_not(is_role))
    def _():
        pl.semaphore_wait(barrier, base + (nx - 1) * 3)

    @pl.when(jnp.logical_not(is_early))
    def _():
        for y in range(3):
            for d in range(nx):
                pl.semaphore_signal(
                    ready, inc=1, device_id=(lax.rem(xx + d, nx) * nyc + yc, y), device_id_type=MESH
                )

    halo_copies = [
        pltpu.make_async_remote_copy(
            src_ref=pack_ref,
            dst_ref=halo_ref.at[slot],
            send_sem=halo_send.at[slot],
            recv_sem=halo_recv.at[slot],
            device_id=(z, level),
            device_id_type=MESH,
        )
        for slot, z in ((0, right), (1, left))
    ]
    for copy in halo_copies:
        copy.start()

    def copy_a(z, slot):
        return pltpu.make_async_remote_copy(
            src_ref=send_a.at[z],
            dst_ref=recv_a.at[slot],
            send_sem=a_send,
            recv_sem=a_recv,
            device_id=(xx * nyc + z, level),
            device_id_type=MESH,
        )

    def copy_b(x, y):
        return pltpu.make_async_remote_copy(
            src_ref=send_b.at[x],
            dst_ref=recv_b.at[role * nx + xx],
            send_sem=b_send,
            recv_sem=b_recv,
            device_id=(x * nyc + yc, y),
            device_id_type=MESH,
        )

    def copy_d(x, z, y):
        return pltpu.make_async_remote_copy(
            src_ref=send_d.at[z * nx + x],
            dst_ref=recv_d.at[me],
            send_sem=d_send,
            recv_sem=d_recv,
            device_id=(x * nyc + z, y),
            device_id_type=MESH,
        )

    def copy_s(y):
        return pltpu.make_async_remote_copy(
            src_ref=send_s,
            dst_ref=recv_s.at[level],
            send_sem=s_send,
            recv_sem=s_recv,
            device_id=(me, y),
            device_id_type=MESH,
        )

    ny = nyc // 2
    early = list(range(-(-ny // 2))) + list(range(ny - 1, -(-ny // 2) - 1, -1))

    @pl.when(is_high)
    def _():
        send_d[...] = (acc_ref[: 2 * gz, :] + acc_ref[2 * gz :, :]).reshape(send_d.shape)
        for x in range(nx):
            for c in (1, 0):
                copy_d(x, 2 * early[0] + c, 0).start()

    @pl.when(is_role)
    def _():
        binned = acc_ref[: 2 * gz, :] + acc_ref[2 * gz :, :]

        send_a[...] = binned.reshape(send_a.shape)
        recv_a[yc] = send_a[yc]

    @pl.when(is_role)
    def _():
        for d in sorted(range(1, nyc), key=lambda d: -min(d, nyc - d)):
            copy_a(lax.rem(yc + d, nyc), yc).start()

    @pl.when(is_high)
    def _():
        for x in range(nx):
            for c in (1, 0):
                copy_d(x, 2 * early[0] + c, 1).start()
        for y in early[1:]:
            for level_to in range(2):
                for x in range(nx):
                    for c in (1, 0):
                        copy_d(x, 2 * y + c, level_to).start()

    load_s.wait()
    for copy in halo_copies:
        copy.wait_recv()
    merged = jnp.where(lane % 2 == 1, pltpu.roll(halo_ref[0], 1, 1), pltpu.roll(halo_ref[1], LANES - 1, 1))
    zero, one = jnp.zeros((SUB, LANES), F32), jnp.ones((SUB, LANES), F32)
    summaries = []
    for p in range(planes):

        def prepare(b, _, p=p):
            i = p * steps + b
            stiff = load_rows(s_ref, p, b, steps)
            here = load_rows(u_ref, p, b, steps)
            halo = pltpu.roll(merged, LANES - 1 - 2 * i, 1)
            before = jnp.where(lane == 0, halo, pltpu.roll(here, 1, 1))
            after = jnp.where(lane == LANES - 1, halo, pltpu.roll(here, LANES - 1, 1))
            source = here + 0.2 * (after + before - 2.0 * here)
            gain = 1.0 / (1.0 + stiff)
            keep_ref[p, b] = stiff * gain
            gain_ref[p, b] = gain
            gsrc_ref[p, b] = gain * source
            return _

        step_loop(steps, 4, prepare, 0)

    def forward(b, carry):
        out = []
        for p in range(planes):
            value, factor = carry[2 * p : 2 * p + 2]
            keep = keep_ref[p, b]
            value = keep * value + gsrc_ref[p, b]
            factor = keep * factor
            lf_ref[p, b] = value
            ff_ref[p, b] = factor
            out += [value, factor]
        return tuple(out)

    forwards = step_loop(steps, 4, forward, (zero, one) * planes)

    def backward(t, carry):
        out = []
        b = steps - 1 - t
        for p in range(planes):
            value, response, factor = carry[3 * p : 3 * p + 3]
            keep, gain = keep_ref[p, b], gain_ref[p, b]
            value = keep * value + gain * lf_ref[p, b]
            response = keep * response + gain * ff_ref[p, b]
            factor = keep * factor
            at = pl.ds(b, SUB, stride=steps)
            bl_ref[p, at, :] = value
            q_ref[p, at, :] = response
            fb_ref[p, at, :] = factor
            out += [value, response, factor]
        return tuple(out)

    backwards = step_loop(steps, 4, backward, (zero, zero, one) * planes)

    inner = []
    for p in range(planes):
        local_f = forwards[2 * p]
        local_b, response, product = backwards[3 * p : 3 * p + 3]
        pi, li = product, local_f
        for d in (1, 2, 4):
            ok = row >= d
            lp = jnp.where(ok, pltpu.roll(li, d, 0), 0.0)
            pp = jnp.where(ok, pltpu.roll(pi, d, 0), 1.0)
            li, pi = pi * lp + li, pi * pp
        pf = jnp.where(row >= 1, pltpu.roll(pi, 1, 0), 1.0)
        lf = jnp.where(row >= 1, pltpu.roll(li, 1, 0), 0.0)
        pb, cb, qb = product, local_b + response * lf, response * pf
        for d in (1, 2, 4):
            ok = row < SUB - d
            cp = jnp.where(ok, pltpu.roll(cb, SUB - d, 0), 0.0)
            qp = jnp.where(ok, pltpu.roll(qb, SUB - d, 0), 0.0)
            pp = jnp.where(ok, pltpu.roll(pb, SUB - d, 0), 1.0)
            cb, qb, pb = pb * cp + cb, pb * qp + qb, pb * pp
        ok = row < SUB - 1
        summaries.append((pb[0:1], li[SUB - 1 : SUB], cb[0:1], qb[0:1]))
        inner.append(
            (
                pf,
                lf,
                jnp.where(ok, pltpu.roll(pb, SUB - 1, 0), 1.0),
                jnp.where(ok, pltpu.roll(cb, SUB - 1, 0), 0.0),
                jnp.where(ok, pltpu.roll(qb, SUB - 1, 0), 0.0),
            )
        )
    own_alpha = jnp.concatenate([1.0 / keep_ref[p, 0, 0:1] for p in range(planes)], axis=0)
    own_eps = jnp.concatenate([1.0 / s_ref[p, levels - 1 : levels, :] for p in range(planes)], axis=0)
    at_bottom, at_top = level == 0, level == gy - 1
    blocks = [jnp.concatenate([summaries[p][c] for p in range(planes)], axis=0) for c in range(4)]
    blocks[0] = blocks[0] * jnp.where(at_bottom, own_alpha, jnp.where(at_top, own_eps, 1.0))
    summary = jnp.concatenate(blocks, axis=0)
    send_s[...] = summary
    recv_s[level] = summary

    def summary_to(levels_to):
        for y in levels_to:

            @pl.when(level != y)
            def _(y=y):
                copy_s(y).start()

    def second_to(levels_to):
        for y in levels_to:
            for d in sorted(range(1, nx), key=lambda d: -min(d, nx - d)):
                copy_b(lax.rem(xx + d, nx), y).start()

            @pl.when(level != y)
            def _(y=y):
                copy_b(xx, y).start()

    summary_to(range(3))

    @pl.when(jnp.logical_not(is_early))
    def _():
        summary_to(range(3, gy))

    @pl.when(is_role)
    def _():
        pltpu.make_async_copy(recv_a.at[pl.ds(0, nyc - 1)], recv_a.at[pl.ds(0, nyc - 1)], a_recv).wait()
        part = recv_a[0]
        for i in range(1, nyc):
            part = part + recv_a[i]
        for x in range(nx):
            send_b[x] = part[2 * x : 2 * x + 2, :]
        recv_b[role * nx + xx] = send_b[xx]

    @pl.when(is_early)
    def _():
        second_to(range(3))
        pl.semaphore_wait(ready, nx * (gy - 3))
        summary_to(range(3, gy))
        second_to(range(3, gy))

    @pl.when(is_high)
    def _():
        second_to(range(2, gy))

    pltpu.make_async_copy(recv_s.at[pl.ds(0, gy - 1)], recv_s.at[pl.ds(0, gy - 1)], s_recv).wait()

    def block(g, c):
        return recv_s[g, 2 * c : 2 * c + 2, :]

    alphas, betas = [None, block(0, 0)], [None, block(0, 1)]
    for g in range(1, gy - 1):
        alphas.append(block(g, 0) * alphas[g])
        betas.append(block(g, 0) * betas[g] + block(g, 1))
    alpha, beta = jnp.where(at_bottom, own_alpha, 0.0), jnp.zeros_like(own_alpha)
    for g in range(1, gy):
        alpha = jnp.where(level == g, alphas[g], alpha)
        beta = jnp.where(level == g, betas[g], beta)
    top = gy - 1
    gam, dlt, eps = block(top, 3) * alphas[top], block(top, 2) + block(top, 3) * betas[top], block(top, 0)
    gamma, delta = jnp.zeros_like(own_alpha), jnp.zeros_like(own_alpha)
    epsilon = jnp.where(at_top, own_eps, 0.0)
    for g in range(gy - 2, -1, -1):
        gamma = jnp.where(level == g, gam, gamma)
        delta = jnp.where(level == g, dlt, delta)
        epsilon = jnp.where(level == g, eps, epsilon)
        if g:
            gam = block(g, 0) * gam + block(g, 3) * alphas[g]
            dlt = block(g, 0) * dlt + block(g, 2) + block(g, 3) * betas[g]
            eps = block(g, 0) * eps

    def arrive(slots):
        pltpu.make_async_copy(recv_b.at[pl.ds(0, slots)], recv_b.at[pl.ds(0, slots)], b_recv).wait()

    def gather(r):
        total = recv_b[r * nx]
        for x in range(1, nx):
            total = total + recv_b[r * nx + x]
        return total

    @pl.when(is_direct)
    def _():
        arrive(3 * nx - 1)
        pltpu.make_async_copy(recv_d, recv_d, d_recv).wait()
        parts = [recv_d[i] for i in range(4)]
        for i in range(4, gz):
            parts[i % 4] = parts[i % 4] + recv_d[i]
        high_ref[...] = (parts[0] + parts[1]) + (parts[2] + parts[3])

    @pl.when(is_role & jnp.logical_not(is_direct))
    def _():
        arrive(4 * nx - 1)
        high_ref[...] = gather(3)

    @pl.when(jnp.logical_not(is_role))
    def _():
        arrive(4 * nx)
        high_ref[...] = gather(3)

    stress_low = gather(0) / jnp.maximum(gather(2), 1.0)
    stress_top = high_ref[...] / jnp.maximum(gather(1), 1.0)
    f_in = alpha * stress_low + beta
    b_in = gamma * stress_low + delta + epsilon * stress_top
    for p in range(planes):
        pf, lf, pb, cb, qb = inner[p]
        below = pf * f_in[p : p + 1] + lf
        above = pb * b_in[p : p + 1] + cb + qb * f_in[p : p + 1]

        for j in range(SUB):
            cut = slice(j * steps, (j + 1) * steps)
            out_ref[p, cut, :] = (
                bl_ref[p, cut, :] + q_ref[p, cut, :] * below[j : j + 1] + fb_ref[p, cut, :] * above[j : j + 1]
            )

    for copy in halo_copies:
        copy.wait_send()
    pltpu.make_async_copy(recv_s.at[pl.ds(0, gy - 1)], recv_s.at[pl.ds(0, gy - 1)], s_send).wait()

    @pl.when(is_role)
    def _():
        left_a, left_b = send_a.at[pl.ds(0, nyc - 1)], send_b.at[pl.ds(0, nx - 1)]
        pltpu.make_async_copy(left_a, left_a, a_send).wait()
        pltpu.make_async_copy(left_b, left_b, b_send).wait()
        for _ in range(gy - 3):
            pltpu.make_async_copy(send_b, send_b, b_send).wait()

    @pl.when(is_early)
    def _():
        for _ in range(2):
            pltpu.make_async_copy(send_b, send_b, b_send).wait()

    @pl.when(is_high)
    def _():
        for _ in range(2):
            pltpu.make_async_copy(send_d, send_d, d_send).wait()


def local(gz, gy, nx, *args):
    u, v, w, s, w_in, b_in, w_mid, b_mid, w_out, cell, height, face, owner = args
    planes, levels, span = u.shape
    steps = levels // SUB
    nyc = gz // nx
    rows = cell.shape[1]
    vmem = pltpu.VMEM
    scratch = [
        vmem(u.shape, F32),
        vmem(u.shape, F32),
        vmem((2, planes, WIN, span), F32),
        vmem((3, span), F32),
        vmem((3, 1, span), F32),
        vmem((span, span), F32),
        vmem((2, rows), jnp.int32),
        vmem((2, rows), jnp.int32),
        vmem((2, rows), jnp.int32),
        vmem((1, 2 * rows), jnp.int32),
        vmem((6, span, span), F32),
        vmem((2 * span, 2 * span), BF16),
        vmem((3, planes * HMAX, span), F32),
        vmem((planes * HMAX, span), F32),
        vmem((4 * gz, span), F32),
        vmem((planes, steps, SUB, span), F32),
        vmem((planes, steps, SUB, span), F32),
        vmem((planes, steps, SUB, span), F32),
        vmem((planes, steps, SUB, span), F32),
        vmem((planes, steps, SUB, span), F32),
        vmem(u.shape, F32),
        vmem(u.shape, F32),
        vmem(u.shape, F32),
        vmem((SUB, span), F32),
        vmem((2, SUB, span), F32),
        vmem((nyc, 2 * nx, span), F32),
        vmem((nyc, 2 * nx, span), F32),
        vmem((nx, 2, span), F32),
        vmem((4 * nx, 2, span), F32),
        vmem((gz, 2, span), F32),
        vmem((gz, 2, span), F32),
        vmem((2, span), F32),
        vmem((8, span), F32),
        vmem((gy, 8, span), F32),
        pltpu.SemaphoreType.DMA((13,)),
        pltpu.SemaphoreType.DMA((2,)),
        pltpu.SemaphoreType.DMA((2,)),
    ] + [pltpu.SemaphoreType.DMA] * 8 + [pltpu.SemaphoreType.REGULAR]
    operands = [
        u,
        v,
        w,
        s,
        w_in,
        b_in[None, :],
        w_mid,
        b_mid[None, :],
        w_out[None, :],
        cell,
        height,
        face,
        owner.reshape(1, 2 * rows),
    ]
    return pl.pallas_call(
        functools.partial(kernel, gz, gy, nx),
        out_shape=jax.ShapeDtypeStruct(u.shape, F32),
        in_specs=[pl.BlockSpec(memory_space=pl.ANY)] * 13,
        out_specs=pl.BlockSpec(memory_space=pltpu.VMEM),
        scratch_shapes=scratch,
        compiler_params=pltpu.CompilerParams(
            collective_id=0, has_side_effects=True, vmem_limit_bytes=40 * 2**20
        ),
    )(*[pltpu.with_memory_space_constraint(x, pltpu.HBM) for x in operands])


def solution(mesh):
    field = P(None, "gy", "gz")
    gz, gy = mesh.shape["gz"], mesh.shape["gy"]
    return jax.shard_map(
        functools.partial(local, gz, gy, 4),
        mesh=mesh,
        in_specs=(field,) * 4 + (P(),) * 5 + (P(None, "gz"),) * 3 + (P(None, "gz", None),),
        out_specs=field,
        check_vma=False,
    )
```
